512 devices in a mesh: band: 32 (over z, y_lo), grid: 16 (over x, y_hi, core).
Axes of the slice: x: 4, y: 4 (y_hi: 2, y_lo: 2; y = y_hi * 2 + y_lo), z: 16, core: 2. Of those that a mesh axis runs over, the one named last changes fastest.
Arguments:
- orbitals: float32 [128, 128, 128, 128], P('band', 'grid'), may hold values from -6 to 6
- spin_channel: int32 [128], replicated, may hold values from 0 to 1
Outputs:
- exchange_action: float32 [128, 128, 128, 128], P('band', 'grid')
The draws below stay inside these ranges and needn't reach their ends.
All inputs are finite; a program needn't handle non-finite values.
Results may differ from the reference program's by a relative error of at most 0.0003.
Values sent between devices are 32-bit elements; how exact they have to be, the bound alone decides.
No kernel may reach another device: no remote copies, remote signals or barrier semaphores. Data moves between devices by JAX's collectives and lax.ppermute only.
A program may use at most 64 MiB of HBM per device.

```python
import math
import jax
import jax.numpy as jnp
from jax import lax

NX = 128
NY = 128
NZ = 128
NB = 4
PARTNER_BIT = 2
NORB = 128
N_BAND = 32


def with_ends(drawn, rng, smallest, largest):
    dims = drawn.shape
    spot = [jax.random.randint(jax.random.fold_in(rng, axis), (), 0, dims[axis]) for axis in range(len(dims))]
    drawn = drawn.at[tuple(spot)].set(smallest)
    longest = dims.index(max(dims))
    spot[longest] = (spot[longest] + 1) % dims[longest]
    return drawn.at[tuple(spot)].set(largest)


def block_levels(key, shape, pieces, smallest, top_value):
    def one(dim, shards_of):
        heights = jax.random.uniform(jax.random.fold_in(jax.random.fold_in(key, 6), dim), (shards_of,), jnp.float32, smallest / len(pieces), top_value / len(pieces))
        return jnp.repeat(jnp.exp(heights), shape[dim] // shards_of).reshape((-1,) + (1,) * (len(shape) - dim - 1))

    loudness = one(*pieces[0])
    for cut in pieces[1:]:
        loudness = loudness * one(*cut)
    return loudness


def centred(rng, extent, spread, reach, pieces=(), kind=jnp.bfloat16):
    values = jax.random.normal(rng, extent, jnp.float32) * spread
    if len(pieces) > 0:
        values = block_levels(rng, extent, pieces, -0.22, 0.18) * values
    return jnp.clip(values, min=-reach, max=reach).astype(kind)


def setup_inputs(seed: int = 0) -> dict:
    keys = jax.random.split(jax.random.key(seed), 3)
    return {
        "orbitals": centred(keys[0], (NORB, NX, NY, NZ), 1.0, 6.0, ((0, 32), (1, 16)), jnp.float32),
        "spin_channel": with_ends(jax.random.randint(keys[1], (NORB,), 0, 2), jax.random.fold_in(keys[1], 1), 0, 1).astype(jnp.int32),
    }


def signed(number, length):
    return jnp.where(number < length // 2, number, number - length)

def coulomb_half():
    strength = math.sqrt(NX * NY * NZ) / 4.0
    along_x = signed(jnp.arange(NX, dtype=jnp.int32), NX)
    along_y = signed(jnp.arange(NY, dtype=jnp.int32), NY)
    along_z = jnp.arange(NZ // 2 + 1, dtype=jnp.int32)
    squared = along_x[:, None, None] ** 2 + along_y[None, :, None] ** 2 + along_z[None, None, :] ** 2
    bounded = jnp.maximum(squared, 1).astype(jnp.float32)
    return jnp.where(squared == 0, jnp.float32(0.0), jnp.float32(strength) / bounded)

def reference(orbitals, spin_channel):
    kernel = coulomb_half()
    blocks = orbitals.reshape(N_BAND, NB, NX, NY, NZ)
    spin_blocks = spin_channel.reshape(N_BAND, NB)
    flip_bit = 2 ** PARTNER_BIT

    def one_group(band_group):
        partner = jnp.bitwise_xor(band_group, flip_bit).astype(jnp.int32)
        own_block = blocks[band_group]
        other_block = blocks[partner]
        own_spin = spin_blocks[band_group]
        other_spin = spin_blocks[partner]

        def one_partner(running, number):
            partner_orbital = other_block[number]
            same_spin = (own_spin == other_spin[number]).astype(jnp.float32)
            density = own_block * partner_orbital[None] * same_spin[:, None, None, None]
            spectrum = jnp.fft.rfftn(density, axes=(1, 2, 3))
            potential = jnp.fft.irfftn(kernel * spectrum, s=(NX, NY, NZ), axes=(1, 2, 3))
            return (running - potential * partner_orbital[None], None)
        running, _ = lax.scan(one_partner, jnp.zeros_like(own_block), jnp.arange(NB, dtype=jnp.int32))
        return running
    result = lax.map(one_group, jnp.arange(N_BAND, dtype=jnp.int32))
    return result.reshape(N_BAND * NB, NX, NY, NZ)
```

```python
import math

import jax
import jax.numpy as jnp
import numpy as np
from jax import lax
from jax.experimental import pallas as pl
from jax.experimental.pallas import tpu as pltpu
from jax.sharding import PartitionSpec as P

PARTNER_BIT = 2
ORBITALS = 4
LANES = 128
PLANES = 8
VMEM_BYTES = 40 * 2**20


def fourier_tables(length, planes):
    number = np.arange(length)
    angles = (number[:, None] * number[None, :] % length) * (2.0 * math.pi / length)
    cosine, sine = np.cos(angles), np.sin(angles)
    plus = np.block([[cosine, -sine], [sine, cosine]])
    minus = plus.T
    blocks = length // planes
    order = np.arange(2 * length).reshape(2, blocks, planes).transpose(1, 0, 2).reshape(-1)
    return plus, plus[:, order], minus, minus[order, :]


def two_parts(table):
    exact = jnp.asarray(table.astype(np.float32))
    high = exact.astype(jnp.bfloat16)
    low = (exact - high.astype(jnp.float32)).astype(jnp.bfloat16)
    return jnp.stack([high, low])


def split(value):
    high = value.astype(jnp.bfloat16)
    return high, (value - high.astype(jnp.float32)).astype(jnp.bfloat16)


def dot(a, b):
    return jnp.dot(a, b, preferred_element_type=jnp.float32)


def from_left(table_ref, value):
    high, low = split(value)
    return dot(table_ref[0], high) + dot(table_ref[0], low) + dot(table_ref[1], high)


def from_right(value, table_ref):
    high, low = split(value)
    return dot(high, table_ref[0]) + dot(low, table_ref[0]) + dot(high, table_ref[1])


def forward_kernel(choice, spin, u_ref, vw_ref, right_ref, left_ref, out_ref):
    planes = u_ref.shape[0]
    size = u_ref.shape[1]
    s0, s1 = spin[0], spin[1]
    rows = []
    for x in range(planes):
        u = u_ref[x]
        rows.append(jnp.concatenate([u * vw_ref[0, x] * s0, u * vw_ref[1, x] * s1], axis=1))
    along_z = from_right(jnp.concatenate(rows, axis=0), right_ref)
    columns = []
    for x in range(planes):
        part = along_z[x * size:(x + 1) * size]
        columns.append(jnp.concatenate([part[:, :LANES], part[:, LANES:]], axis=0))
    along_y = from_left(left_ref, jnp.concatenate(columns, axis=1))
    blocks = out_ref.shape[0]
    for x in range(planes):
        for c in range(2):
            block = along_y[c * size:(c + 1) * size, x * LANES:(x + 1) * LANES]
            out_ref[:, c, x] = block.reshape(blocks, size // blocks, LANES)


def solve_kernel(in_ref, kernel_ref, left_ref, right_ref, out_ref):
    columns = kernel_ref.shape[0]
    rows = in_ref.shape[0] // columns
    for y in range(0, columns, 2):
        value = jnp.concatenate([in_ref[pl.ds(y + k, rows, stride=columns), :] for k in range(2)], axis=1)
        weight = jnp.concatenate([kernel_ref[y], kernel_ref[y + 1]], axis=1)
        spectrum = from_left(left_ref, value) * jnp.concatenate([weight, weight], axis=0)
        solved = from_left(right_ref, spectrum)
        for k in range(2):
            out_ref[pl.ds(y + k, rows, stride=columns), :] = solved[:, k * LANES:(k + 1) * LANES]


def inverse_kernel(
    choice, spin, in_ref, u_ref, vw_ref, before_ref, sum_ref, left_ref, right_ref, total_ref, back_ref
):
    planes = u_ref.shape[0]
    size = u_ref.shape[1]
    s0, s1, keep = spin[0], spin[1], spin[2]
    columns = []
    for x in range(planes):
        parts = [in_ref[:, c, x].reshape(size, LANES) for c in range(2)]
        columns.append(jnp.concatenate(parts, axis=0))
    along_y = from_left(left_ref, jnp.concatenate(columns, axis=1))
    rows = []
    for x in range(planes):
        part = along_y[:, x * LANES:(x + 1) * LANES]
        rows.append(jnp.concatenate([part[:size], part[size:]], axis=1))
    potential = from_right(jnp.concatenate(rows, axis=0), right_ref)
    for x in range(planes):
        part = potential[x * size:(x + 1) * size]
        v0 = part[:, :LANES] * s0
        v1 = part[:, LANES:] * s1
        u = u_ref[x]
        total_ref[0, x] = sum_ref[0, x] - v0 * u
        total_ref[1, x] = sum_ref[1, x] - v1 * u
        back_ref[x] = before_ref[x] * keep - (v0 * vw_ref[0, x] + v1 * vw_ref[1, x])


def add_kernel(choice, more_ref, sum_ref, total_ref):
    total_ref[0] = sum_ref[0] + more_ref[...]


def params():
    return pltpu.CompilerParams(dimension_semantics=("arbitrary",), vmem_limit_bytes=VMEM_BYTES)


STEP = 2


def forward(choice, spin, u, orbitals, right, left, blocks):
    planes, size, lanes = u.shape
    table = pl.BlockSpec((2, 2 * size, 2 * size), lambda i, c, s: (0, 0, 0))
    return pl.pallas_call(
        forward_kernel,
        grid_spec=pltpu.PrefetchScalarGridSpec(
            num_scalar_prefetch=2,
            grid=(planes // STEP,),
            in_specs=[
                pl.BlockSpec((STEP, size, lanes), lambda i, c, s: (i, 0, 0)),
                pl.BlockSpec((2, STEP, size, lanes), lambda i, c, s: (c[0], i, 0, 0)),
                table,
                table,
            ],
            out_specs=pl.BlockSpec((blocks, 2, STEP, size // blocks, lanes), lambda i, c, s: (0, 0, i, 0, 0)),
        ),
        out_shape=jax.ShapeDtypeStruct((blocks, 2, planes, size // blocks, lanes), jnp.float32),
        compiler_params=params(),
        name="forward_planes",
    )(choice, spin, u, orbitals, right, left)


def solve(field, kernel, left, right):
    blocks, two, planes, columns, lanes = field.shape
    flat = (blocks * two * planes * columns, lanes)
    solved = pl.pallas_call(
        solve_kernel,
        out_shape=jax.ShapeDtypeStruct(flat, jnp.float32),
        compiler_params=pltpu.CompilerParams(vmem_limit_bytes=VMEM_BYTES),
        name="solve_columns",
    )(field.reshape(flat), kernel, left, right)
    return solved.reshape(field.shape)


def inverse(choice, spin, field, u, orbitals, before, total, left, right):
    planes, size, lanes = u.shape
    blocks = field.shape[0]
    table = pl.BlockSpec((2, 2 * size, 2 * size), lambda i, c, s: (0, 0, 0))
    plane = pl.BlockSpec((STEP, size, lanes), lambda i, c, s: (i, 0, 0))
    pair = pl.BlockSpec((2, STEP, size, lanes), lambda i, c, s: (c[0], i, 0, 0))
    return pl.pallas_call(
        inverse_kernel,
        grid_spec=pltpu.PrefetchScalarGridSpec(
            num_scalar_prefetch=2,
            grid=(planes // STEP,),
            in_specs=[
                pl.BlockSpec((blocks, 2, STEP, size // blocks, lanes), lambda i, c, s: (0, 0, i, 0, 0)),
                plane,
                pair,
                plane,
                pair,
                table,
                table,
            ],
            out_specs=[pair, plane],
        ),
        out_shape=[
            jax.ShapeDtypeStruct(total.shape, jnp.float32),
            jax.ShapeDtypeStruct(u.shape, jnp.float32),
        ],
        input_output_aliases={6: 0},
        compiler_params=params(),
        name="inverse_planes",
    )(choice, spin, field, u, orbitals, before, total, left, right)


def add_into(choice, total, more):
    planes, size, lanes = more.shape
    one = pl.BlockSpec((1, STEP, size, lanes), lambda i, c: (c[0], i, 0, 0))
    return pl.pallas_call(
        add_kernel,
        grid_spec=pltpu.PrefetchScalarGridSpec(
            num_scalar_prefetch=1,
            grid=(planes // STEP,),
            in_specs=[pl.BlockSpec((STEP, size, lanes), lambda i, c: (i, 0, 0)), one],
            out_specs=one,
        ),
        out_shape=jax.ShapeDtypeStruct(total.shape, jnp.float32),
        input_output_aliases={2: 0},
        compiler_params=params(),
        name="add_received",
    )(choice, more, total)


def signed(number, length):
    return jnp.where(number < length // 2, number, number - length)


def coulomb_block(size, column_count, first_column):
    strength = math.sqrt(size**3) / 4.0
    along_x = signed(jnp.arange(size, dtype=jnp.int32), size)
    along_y = signed(first_column + jnp.arange(column_count, dtype=jnp.int32), size)
    squared = along_y[:, None, None] ** 2 + along_x[None, :, None] ** 2 + along_x[None, None, :] ** 2
    bounded = jnp.maximum(squared, 1).astype(jnp.float32)
    kernel = jnp.where(squared == 0, jnp.float32(0.0), jnp.float32(strength) / bounded)
    return kernel * jnp.float32(1.0 / size**3)


def role_of(group):
    return ((group >> PARTNER_BIT) ^ (group >> (PARTNER_BIT - 1))) & 1


def exchange(field):
    return lax.all_to_all(field, "grid", split_axis=0, concat_axis=0, tiled=True)


def shards(orbitals, spin_channel):
    count, planes, size, lanes = orbitals.shape
    grid_size = lax.axis_size("grid")
    groups = lax.axis_size("band")
    band = lax.axis_index("band")
    partner = band ^ (1 << PARTNER_BIT)
    role = role_of(band)
    first = role == 0
    every = [(g, g ^ (1 << PARTNER_BIT)) for g in range(groups)]
    to_first = [(g, p) for g, p in every if role_of(p) == 0]
    to_second = [(g, p) for g, p in every if role_of(p) == 1]

    own_spin = lax.dynamic_slice_in_dim(spin_channel, band * count, count)
    other_spin = lax.dynamic_slice_in_dim(spin_channel, partner * count, count)

    plus, plus_x, minus, minus_x = (two_parts(t) for t in fourier_tables(size, planes))
    kernel = coulomb_block(size, size // grid_size, lax.axis_index("grid") * (size // grid_size))

    def index(a, b):
        return jnp.where(first, a, b).astype(jnp.int32)

    def orbital(number):
        return lax.dynamic_index_in_dim(orbitals, number, 0, keepdims=False)

    received = []
    for k in range(ORBITALS):
        if k % 2 == 0:
            sent = orbital(index(2 + k // 2, k))
        else:
            sent = orbitals[k]
        if received:
            sent, received[-1] = lax.optimization_barrier((sent, received[-1]))
        received.append(lax.ppermute(sent, "band", every if k % 2 == 0 else to_first))

    chosen, spins, us = [], [], []
    for k in range(ORBITALS):
        pair = index(0, k % 2)
        chosen.append(pair.reshape(1))
        far = other_spin[index(k, 2 + k // 2)]
        near = lax.dynamic_slice_in_dim(own_spin, 2 * pair, 2)
        same = (near == far).astype(jnp.float32)
        keep = index(0, k % 2).astype(jnp.float32)
        spins.append(jnp.concatenate([same, keep.reshape(1)]))
        us.append(received[k] if k % 2 == 0 else jnp.where(first, received[k], received[k - 1]))

    def planes_of(k):
        return forward(chosen[k], spins[k], us[k], orbitals, minus, plus, grid_size)

    total = jnp.zeros_like(orbitals)
    before = jnp.zeros_like(us[0])
    returned = []
    ahead = planes_of(0)
    arrived = exchange(ahead)
    for k in range(ORBITALS):
        solved = solve(arrived, kernel, plus_x, minus_x)
        if k + 1 < ORBITALS:
            both = exchange(jnp.concatenate([planes_of(k + 1), solved], axis=1))
            arrived, back = both[:, :2], both[:, 2:]
        else:
            back = exchange(solved)
        total, before = inverse(
            chosen[k], spins[k], back, us[k], orbitals, before, total, minus, plus
        )
        returned.append(lax.ppermute(before, "band", every if k % 2 == 1 else to_second))
    for k in range(ORBITALS):
        place = index(2 + k // 2, k)
        total = add_into(place.reshape(1), total, returned[k])
    return total


def solution(mesh):
    return jax.shard_map(
        shards,
        mesh=mesh,
        in_specs=(P("band", "grid", None, None), P()),
        out_specs=P("band", "grid", None, None),
        check_vma=False,
    )
```

```python
import math

import jax
import jax.numpy as jnp
import numpy as np
from jax import lax
from jax.experimental import pallas as pl
from jax.experimental.pallas import tpu as pltpu
from jax.sharding import PartitionSpec as P

PARTNER_BIT = 2
ORBITALS = 4
LANES = 128
VMEM_BYTES = 40 * 2**20
EARLY = pl.CostEstimate(flops=0, bytes_accessed=200 * 10**6, transcendentals=0)
ROUNDS = 3
ENTRY = 8


def cover(rows, columns, rounds):
    cells = [
        (i, j) for i in range(ORBITALS) for j in range(ORBITALS) if (i < rows) == (j < columns)
    ]

    def search(left, first, second):
        if not left:
            return first, second
        i, j = left[0]
        below = [r for r, c in left if c == j and r != i]
        beside = [c for r, c in left if r == i and c != j]
        options = [(0, r) for r in below] + [(1, c) for c in beside] + [(0, None), (1, None)]
        for side, other in options:
            if len((first, second)[side]) == rounds:
                continue
            taken = {(i, j)}
            if other is not None:
                taken.add((other, j) if side == 0 else (i, other))
            own, far = (i, j) if side == 0 else (j, i)
            entry = (far, own, (own + 1) % ORBITALS if other is None else other, int(other is not None))
            rest = [c for c in left if c not in taken]
            found = search(
                rest,
                first + [entry] if side == 0 else first,
                second + [entry] if side == 1 else second,
            )
            if found is not None:
                return found
        return None

    return search(cells, [], [])


def plan_table():
    patterns = 2**ORBITALS
    bits = [[(p >> i) & 1 for i in range(ORBITALS)] for p in range(patterns)]
    order = [sorted(range(ORBITALS), key=lambda i: b[i]) for b in bits]
    zeros = [b.count(0) for b in bits]
    found = {}
    for rows in range(ORBITALS + 1):
        for columns in range(ORBITALS + 1):
            found[rows, columns] = cover(rows, columns, ROUNDS) or cover(rows, columns, ROUNDS + 1)
    table = np.zeros((2, patterns, patterns, ROUNDS + 1, ENTRY), np.int32)
    table[..., 1] = 1
    for side in range(2):
        for own in range(patterns):
            for other in range(patterns):
                first, second = (own, other) if side == 0 else (other, own)
                both = found[zeros[first], zeros[second]]
                for number, (_, a, b, mask) in enumerate(both[side]):
                    table[side, own, other, number, :4] = (order[own][a], order[own][b], 1, mask)
                for number, (u, *_) in enumerate(both[1 - side]):
                    table[side, own, other, number, 4] = order[own][u]
    rows = np.zeros((2 * patterns * patterns, 1, LANES), np.int32)
    rows[:, 0, :(ROUNDS + 1) * ENTRY] = table.reshape(2 * patterns * patterns, -1)
    return rows


def plan_kernel(spin, table_ref, orbitals_ref, plan_ref, sent_ref, row_ref, sems):
    band = lax.axis_index("band")
    partner = band ^ (1 << PARTNER_BIT)
    row = (band >> PARTNER_BIT) & 1
    for group in (band, partner):
        own = jnp.int32(0)
        for i in range(ORBITALS):
            own = own + spin[group * ORBITALS + i] * (1 << i)
        row = row * 2**ORBITALS + own
    copy = pltpu.make_async_copy(table_ref.at[row], row_ref, sems.at[0])
    copy.start()
    copy.wait()
    copy = pltpu.make_async_copy(orbitals_ref.at[row_ref[0, 4]], sent_ref, sems.at[1])
    copy.start()
    for i in range((ROUNDS + 1) * ENTRY):
        plan_ref[i] = row_ref[0, i]
    copy.wait()


def make_plan(spin_channel, orbitals):
    smem = pl.BlockSpec(memory_space=pltpu.SMEM)
    hbm = pl.BlockSpec(memory_space=pl.ANY)
    return pl.pallas_call(
        plan_kernel,
        in_specs=[smem, hbm, hbm],
        out_specs=[smem, pl.BlockSpec(memory_space=pltpu.VMEM)],
        out_shape=[
            jax.ShapeDtypeStruct(((ROUNDS + 1) * ENTRY,), jnp.int32),
            jax.ShapeDtypeStruct(orbitals.shape[1:], jnp.float32),
        ],
        scratch_shapes=[pltpu.SMEM((1, LANES), jnp.int32), pltpu.SemaphoreType.DMA((2,))],
        name="plan_rounds",
    )(spin_channel, jnp.asarray(plan_table()), orbitals)


def needs_more(spin_channel):
    flip = 1 << PARTNER_BIT
    ones = jnp.sum(spin_channel.reshape(-1, 2, flip, ORBITALS), axis=(1, 3))
    return jnp.any((ones == 0) | (ones == 2 * ORBITALS))


def fourier_tables(length, planes):
    number = np.arange(length)
    angles = (number[:, None] * number[None, :] % length) * (2.0 * math.pi / length)
    cosine, sine = np.cos(angles), np.sin(angles)
    plus = np.block([[cosine, -sine], [sine, cosine]])
    minus = plus.T
    blocks = length // planes
    order = np.arange(2 * length).reshape(2, blocks, planes).transpose(1, 0, 2).reshape(-1)
    return plus, plus[:, order], minus, minus[order, :]


def two_parts(table):
    exact = table.astype(np.float32)
    high = exact.astype(jnp.bfloat16)
    low = (exact - high.astype(np.float32)).astype(jnp.bfloat16)
    return jnp.asarray(np.stack([high, low]))


def split(value):
    high = value.astype(jnp.bfloat16)
    return high, (value - high.astype(jnp.float32)).astype(jnp.bfloat16)


def dot(a, b):
    return jnp.dot(a, b, preferred_element_type=jnp.float32)


def from_left(table_ref, value):
    high, low = split(value)
    return dot(table_ref[0], high) + dot(table_ref[0], low) + dot(table_ref[1], high)


def from_right(value, table_ref):
    high, low = split(value)
    return dot(high, table_ref[0]) + dot(low, table_ref[0]) + dot(high, table_ref[1])


def forward_kernel(number, plan, u_ref, v_ref, w_ref, right_ref, left_ref, out_ref):
    planes, size = u_ref.shape[:2]
    blocks = out_ref.shape[0]
    s0 = plan[number * ENTRY + 2].astype(jnp.float32)
    s1 = plan[number * ENTRY + 3].astype(jnp.float32)
    for first in range(0, planes, 2):
        rows = []
        for x in range(first, first + 2):
            u = u_ref[x]
            rows.append(jnp.concatenate([u * v_ref[0, x] * s0, u * w_ref[0, x] * s1], axis=1))
        along_z = from_right(jnp.concatenate(rows, axis=0), right_ref)
        columns = []
        for k in range(2):
            part = along_z[k * size:(k + 1) * size]
            columns.append(jnp.concatenate([part[:, :LANES], part[:, LANES:]], axis=0))
        along_y = from_left(left_ref, jnp.concatenate(columns, axis=1))
        for k in range(2):
            for c in range(2):
                block = along_y[c * size:(c + 1) * size, k * LANES:(k + 1) * LANES]
                out_ref[:, c, first + k] = block.reshape(blocks, size // blocks, LANES)


def solve_kernel(in_ref, kernel_ref, left_ref, right_ref, *rest):
    out_ref = rest[-1]
    columns = kernel_ref.shape[0]
    rows = math.prod(in_ref.shape[:3])
    flat_in = in_ref.reshape(rows * columns, LANES)
    flat_out = out_ref.reshape(rows * columns, LANES)
    for y in range(0, columns, 2):
        value = jnp.concatenate([flat_in[pl.ds(y + k, rows, stride=columns), :] for k in range(2)], axis=1)
        weight = jnp.concatenate([kernel_ref[y], kernel_ref[y + 1]], axis=1)
        spectrum = from_left(left_ref, value) * jnp.concatenate([weight, weight], axis=0)
        solved = from_left(right_ref, spectrum)
        for k in range(2):
            flat_out[pl.ds(y + k, rows, stride=columns), :] = solved[:, k * LANES:(k + 1) * LANES]


def inverse_kernel(number, plan, in_ref, u_ref, v_ref, w_ref, left_ref, right_ref, own_ref, back_ref):
    planes, size = u_ref.shape[:2]
    s0 = plan[number * ENTRY + 2].astype(jnp.float32)
    s1 = plan[number * ENTRY + 3].astype(jnp.float32)
    for first in range(0, planes, 2):
        columns = []
        for x in range(first, first + 2):
            columns.append(jnp.concatenate([in_ref[:, c, x].reshape(size, LANES) for c in range(2)], axis=0))
        along_y = from_left(left_ref, jnp.concatenate(columns, axis=1))
        rows = []
        for k in range(2):
            part = along_y[:, k * LANES:(k + 1) * LANES]
            rows.append(jnp.concatenate([part[:size], part[size:]], axis=1))
        potential = from_right(jnp.concatenate(rows, axis=0), right_ref)
        for k in range(2):
            x = first + k
            v0 = potential[k * size:(k + 1) * size, :LANES] * s0
            v1 = potential[k * size:(k + 1) * size, LANES:] * s1
            u = u_ref[x]
            own_ref[0, x] = -(v0 * u)
            own_ref[1, x] = -(v1 * u)
            back_ref[x] = -(v0 * v_ref[0, x] + v1 * w_ref[0, x])


def add_kernel(plan, more_ref, sum_ref, total_ref):
    total_ref[...] = sum_ref[...] + more_ref[...]


def in_hbm(value):
    return pltpu.with_memory_space_constraint(value, pltpu.HBM)


def params():
    return pltpu.CompilerParams(dimension_semantics=("arbitrary",), vmem_limit_bytes=VMEM_BYTES)


def whole(shape):
    return pl.BlockSpec(shape, lambda *_: (0,) * len(shape))


def part(shape, place):
    return pl.BlockSpec((shape[0], 2) + shape[2:], lambda *_: (0, place, 0, 0, 0))


def orbital_block(shape, number, field):
    return pl.BlockSpec((1,) + shape[1:], lambda i, plan: (plan[number * ENTRY + field], 0, 0, 0))


def forward(number, width, plan, u, orbitals, right, left):
    planes, size, lanes = u.shape
    blocks = lax.axis_size("grid")
    shape = (blocks, 2 * width, planes, size // blocks, lanes)
    return pl.pallas_call(
        lambda *refs: forward_kernel(number, *refs),
        grid_spec=pltpu.PrefetchScalarGridSpec(
            num_scalar_prefetch=1,
            grid=(1,),
            in_specs=[
                whole(u.shape),
                orbital_block(orbitals.shape, number, 0),
                orbital_block(orbitals.shape, number, 1),
                whole(right.shape),
                whole(left.shape),
            ],
            out_specs=part(shape, 0),
        ),
        out_shape=pltpu.HBM(shape, jnp.float32),
        cost_estimate=EARLY if number else None,
        compiler_params=params(),
        name="forward_planes",
    )(plan, u, orbitals, orbitals, right, left)


def solve(arrived, kernel, left, right, ahead, after):
    hbm = pl.BlockSpec(memory_space=pl.ANY)
    operands = [in_hbm(arrived), kernel, left, right]
    specs = [part(arrived.shape, 0), whole(kernel.shape), whole(left.shape), whole(right.shape)]
    if ahead is None:
        shape, place, aliases = (arrived.shape[0], 2) + arrived.shape[2:], 0, {}
    else:
        shape, place, aliases = ahead.shape, 1, {len(operands): 0}
        operands.append(in_hbm(ahead))
        specs.append(hbm)
    return pl.pallas_call(
        solve_kernel,
        grid=(1,),
        in_specs=specs + [hbm] * len(after),
        out_specs=part(shape, place),
        out_shape=pltpu.HBM(shape, jnp.float32),
        input_output_aliases=aliases,
        compiler_params=params(),
        name="solve_columns",
    )(*operands, *after)


def inverse(number, place, plan, arrived, u, orbitals, left, right):
    own = (2,) + u.shape
    return pl.pallas_call(
        lambda *refs: inverse_kernel(number, *refs),
        grid_spec=pltpu.PrefetchScalarGridSpec(
            num_scalar_prefetch=1,
            grid=(1,),
            in_specs=[
                part(arrived.shape, place),
                whole(u.shape),
                orbital_block(orbitals.shape, number, 0),
                orbital_block(orbitals.shape, number, 1),
                whole(left.shape),
                whole(right.shape),
            ],
            out_specs=[whole(own), whole(u.shape)],
        ),
        out_shape=[jax.ShapeDtypeStruct(own, jnp.float32), pltpu.HBM(u.shape, jnp.float32)],
        compiler_params=params(),
        name="inverse_planes",
    )(plan, in_hbm(arrived), u, orbitals, orbitals, left, right)


def add_into(number, field, plan, total, more):
    count = more.shape[0]
    one = (1,) + more.shape[1:]
    target = pl.BlockSpec(one, lambda i, plan: (plan[number * ENTRY + field + i], 0, 0, 0))
    return pl.pallas_call(
        add_kernel,
        grid_spec=pltpu.PrefetchScalarGridSpec(
            num_scalar_prefetch=1,
            grid=(count,),
            in_specs=[pl.BlockSpec(one, lambda i, plan: (i, 0, 0, 0)), target],
            out_specs=target,
        ),
        out_shape=jax.ShapeDtypeStruct(total.shape, jnp.float32),
        input_output_aliases={2: 0},
        compiler_params=params(),
        name="add_terms",
    )(plan, more, total)


def signed(number, length):
    return jnp.where(number < length // 2, number, number - length)


def coulomb_block(size, column_count, first_column):
    strength = math.sqrt(size**3) / 4.0
    along_x = signed(jnp.arange(size, dtype=jnp.int32), size)
    along_y = signed(first_column + jnp.arange(column_count, dtype=jnp.int32), size)
    squared = along_y[:, None, None] ** 2 + along_x[None, :, None] ** 2 + along_x[None, None, :] ** 2
    bounded = jnp.maximum(squared, 1).astype(jnp.float32)
    kernel = jnp.where(squared == 0, jnp.float32(0.0), jnp.float32(strength) / bounded)
    return kernel * jnp.float32(1.0 / size**3)


def exchange(field):
    return lax.all_to_all(field, "grid", split_axis=0, concat_axis=0, tiled=True)


def to_partner(value):
    pairs = [(g, g ^ (1 << PARTNER_BIT)) for g in range(lax.axis_size("band"))]
    return lax.ppermute(value, "band", pairs)


def sent_orbital(number, plan, orbitals):
    return lax.dynamic_index_in_dim(orbitals, plan[number * ENTRY + 4], 0, keepdims=False)


def one_round(number, plan, orbitals, kernel, total, tables):
    plus, plus_x, minus, minus_x = tables
    u = to_partner(sent_orbital(number, plan, orbitals))
    arrived = exchange(forward(number, 1, plan, u, orbitals, minus, plus))
    arrived = exchange(solve(arrived, kernel, plus_x, minus_x, None, ()))
    own, back = inverse(number, 0, plan, arrived, u, orbitals, minus, plus)
    total = add_into(number, 0, plan, total, own)
    return add_into(number, 4, plan, total, to_partner(back)[None])


def shards(orbitals, spin_channel):
    count, planes, size, lanes = orbitals.shape
    column_count = size // lax.axis_size("grid")
    plan, sent = make_plan(spin_channel, orbitals)
    us = [to_partner(sent)]
    kernel = coulomb_block(size, column_count, lax.axis_index("grid") * column_count)
    tables = tuple(two_parts(t) for t in fourier_tables(size, planes))
    plus, plus_x, minus, minus_x = tables
    total = lax.cond(
        needs_more(spin_channel),
        lambda *args: one_round(ROUNDS, *args, jnp.zeros_like(orbitals), tables),
        lambda *args: jnp.zeros_like(orbitals),
        plan, orbitals, kernel,
    )
    for number in range(1, ROUNDS):
        sent, us[-1] = lax.optimization_barrier((sent_orbital(number, plan, orbitals), us[-1]))
        us.append(to_partner(sent))

    def planes_of(number):
        return forward(number, 1 if number == 0 else 2, plan, us[number], orbitals, minus, plus)

    returned = []
    arrived = exchange(planes_of(0))
    for number in range(ROUNDS):
        ahead = planes_of(number + 1) if number + 1 < ROUNDS else None
        after = returned[:max(number - 1, 0)]
        arrived = exchange(solve(arrived, kernel, plus_x, minus_x, ahead, after))
        own, back = inverse(number, 0 if ahead is None else 1, plan, arrived, us[number], orbitals, minus, plus)
        returned.append(to_partner(back))
        total = add_into(number, 0, plan, total, own)
        if number > 0:
            total = add_into(number - 1, 4, plan, total, returned[number - 1][None])
    place = plan[(ROUNDS - 1) * ENTRY + 4]
    last = lax.dynamic_index_in_dim(total, place, 0, keepdims=False) + returned[-1]
    return lax.dynamic_update_index_in_dim(total, last, place, 0)


def solution(mesh):
    return jax.shard_map(
        shards,
        mesh=mesh,
        in_specs=(P("band", "grid", None, None), P()),
        out_specs=P("band", "grid", None, None),
        check_vma=False,
    )
```

```python
import math

import jax
import jax.numpy as jnp
import numpy as np
from jax import lax
from jax.experimental import pallas as pl
from jax.experimental.pallas import tpu as pltpu
from jax.sharding import PartitionSpec as P

PARTNER_BIT = 2
ORBITALS = 4
LANES = 128
VMEM_BYTES = 40 * 2**20
EARLY = pl.CostEstimate(flops=10**11, bytes_accessed=200 * 10**6, transcendentals=0)
ROUNDS = 3
ENTRY = 8


def cover(rows, columns, rounds):
    cells = [
        (i, j) for i in range(ORBITALS) for j in range(ORBITALS) if (i < rows) == (j < columns)
    ]

    def search(left, first, second):
        if not left:
            return first, second
        i, j = left[0]
        below = [r for r, c in left if c == j and r != i]
        beside = [c for r, c in left if r == i and c != j]
        options = [(0, r) for r in below] + [(1, c) for c in beside] + [(0, None), (1, None)]
        for side, other in options:
            if len((first, second)[side]) == rounds:
                continue
            taken = {(i, j)}
            if other is not None:
                taken.add((other, j) if side == 0 else (i, other))
            own, far = (i, j) if side == 0 else (j, i)
            entry = (far, own, (own + 1) % ORBITALS if other is None else other, int(other is not None))
            rest = [c for c in left if c not in taken]
            found = search(
                rest,
                first + [entry] if side == 0 else first,
                second + [entry] if side == 1 else second,
            )
            if found is not None:
                return found
        return None

    return search(cells, [], [])


def plan_table():
    patterns = 2**ORBITALS
    bits = [[(p >> i) & 1 for i in range(ORBITALS)] for p in range(patterns)]
    order = [sorted(range(ORBITALS), key=lambda i: b[i]) for b in bits]
    zeros = [b.count(0) for b in bits]
    found = {}
    for rows in range(ORBITALS + 1):
        for columns in range(ORBITALS + 1):
            found[rows, columns] = cover(rows, columns, ROUNDS) or cover(rows, columns, ROUNDS + 1)
    table = np.zeros((2, patterns, patterns, ROUNDS + 1, ENTRY), np.int32)
    table[..., 1] = 1
    for side in range(2):
        for own in range(patterns):
            for other in range(patterns):
                first, second = (own, other) if side == 0 else (other, own)
                both = found[zeros[first], zeros[second]]
                for number, (_, a, b, mask) in enumerate(both[side]):
                    table[side, own, other, number, :4] = (order[own][a], order[own][b], 1, mask)
                for number, (u, *_) in enumerate(both[1 - side]):
                    table[side, own, other, number, 4] = order[own][u]
    rows = np.zeros((2 * patterns * patterns, 1, LANES), np.int32)
    rows[:, 0, :(ROUNDS + 1) * ENTRY] = table.reshape(2 * patterns * patterns, -1)
    return rows


def plan_kernel(spin, table_ref, orbitals_ref, plan_ref, sent_ref, row_ref, sems):
    band = lax.axis_index("band")
    partner = band ^ (1 << PARTNER_BIT)
    row = (band >> PARTNER_BIT) & 1
    for group in (band, partner):
        own = jnp.int32(0)
        for i in range(ORBITALS):
            own = own + spin[group * ORBITALS + i] * (1 << i)
        row = row * 2**ORBITALS + own
    copy = pltpu.make_async_copy(table_ref.at[row], row_ref, sems.at[0])
    copy.start()
    copy.wait()
    copy = pltpu.make_async_copy(orbitals_ref.at[row_ref[0, 4]], sent_ref, sems.at[1])
    copy.start()
    for i in range((ROUNDS + 1) * ENTRY):
        plan_ref[i] = row_ref[0, i]
    copy.wait()


def make_plan(spin_channel, orbitals):
    smem = pl.BlockSpec(memory_space=pltpu.SMEM)
    hbm = pl.BlockSpec(memory_space=pl.ANY)
    return pl.pallas_call(
        plan_kernel,
        in_specs=[smem, hbm, hbm],
        out_specs=[smem, pl.BlockSpec(memory_space=pltpu.VMEM)],
        out_shape=[
            jax.ShapeDtypeStruct(((ROUNDS + 1) * ENTRY,), jnp.int32),
            jax.ShapeDtypeStruct(orbitals.shape[1:], jnp.float32),
        ],
        scratch_shapes=[pltpu.SMEM((1, LANES), jnp.int32), pltpu.SemaphoreType.DMA((2,))],
        name="plan_rounds",
    )(spin_channel, jnp.asarray(plan_table()), orbitals)


def needs_more(spin_channel):
    flip = 1 << PARTNER_BIT
    ones = jnp.sum(spin_channel.reshape(-1, 2, flip, ORBITALS), axis=(1, 3))
    return jnp.any((ones == 0) | (ones == 2 * ORBITALS))


def fourier_tables(length, planes):
    number = np.arange(length)
    angles = (number[:, None] * number[None, :] % length) * (2.0 * math.pi / length)
    cosine, sine = np.cos(angles), np.sin(angles)
    plus = np.block([[cosine, -sine], [sine, cosine]])
    minus = plus.T
    blocks = length // planes
    order = np.arange(2 * length).reshape(2, blocks, planes).transpose(1, 0, 2).reshape(-1)
    return plus, plus[:, order], minus, minus[order, :]


def two_parts(table):
    exact = table.astype(np.float32)
    high = exact.astype(jnp.bfloat16)
    low = (exact - high.astype(np.float32)).astype(jnp.bfloat16)
    return jnp.asarray(np.stack([high, low]))


def split(value):
    high = value.astype(jnp.bfloat16)
    return high, (value - high.astype(jnp.float32)).astype(jnp.bfloat16)


def dot(a, b):
    return jnp.dot(a, b, preferred_element_type=jnp.float32)


def from_left(table_ref, value):
    high, low = split(value)
    return dot(table_ref[0], high) + dot(table_ref[0], low) + dot(table_ref[1], high)


def from_right(value, table_ref):
    high, low = split(value)
    return dot(high, table_ref[0]) + dot(low, table_ref[0]) + dot(high, table_ref[1])


def forward_kernel(number, plan, u_ref, v_ref, w_ref, right_ref, left_ref, out_ref):
    planes, size = u_ref.shape[:2]
    blocks = out_ref.shape[0]
    s0 = plan[number * ENTRY + 2].astype(jnp.float32)
    s1 = plan[number * ENTRY + 3].astype(jnp.float32)
    for first in range(0, planes, 2):
        rows = []
        for x in range(first, first + 2):
            u = u_ref[x]
            rows.append(jnp.concatenate([u * v_ref[0, x] * s0, u * w_ref[0, x] * s1], axis=1))
        along_z = from_right(jnp.concatenate(rows, axis=0), right_ref)
        columns = []
        for k in range(2):
            part = along_z[k * size:(k + 1) * size]
            columns.append(jnp.concatenate([part[:, :LANES], part[:, LANES:]], axis=0))
        along_y = from_left(left_ref, jnp.concatenate(columns, axis=1))
        for k in range(2):
            for c in range(2):
                block = along_y[c * size:(c + 1) * size, k * LANES:(k + 1) * LANES]
                out_ref[:, c, first + k] = block.reshape(blocks, size // blocks, LANES)


def solve_kernel(in_ref, kernel_ref, left_ref, right_ref, *rest):
    out_ref = rest[-1]
    columns = kernel_ref.shape[0]
    rows = math.prod(in_ref.shape[:3])
    flat_in = in_ref.reshape(rows * columns, LANES)
    flat_out = out_ref.reshape(rows * columns, LANES)
    for y in range(0, columns, 2):
        value = jnp.concatenate([flat_in[pl.ds(y + k, rows, stride=columns), :] for k in range(2)], axis=1)
        weight = jnp.concatenate([kernel_ref[y], kernel_ref[y + 1]], axis=1)
        spectrum = from_left(left_ref, value) * jnp.concatenate([weight, weight], axis=0)
        solved = from_left(right_ref, spectrum)
        for k in range(2):
            flat_out[pl.ds(y + k, rows, stride=columns), :] = solved[:, k * LANES:(k + 1) * LANES]


def inverse_kernel(number, plan, in_ref, u_ref, v_ref, w_ref, left_ref, right_ref, own_ref, back_ref):
    planes, size = u_ref.shape[:2]
    s0 = plan[number * ENTRY + 2].astype(jnp.float32)
    s1 = plan[number * ENTRY + 3].astype(jnp.float32)
    for first in range(0, planes, 2):
        columns = []
        for x in range(first, first + 2):
            columns.append(jnp.concatenate([in_ref[:, c, x].reshape(size, LANES) for c in range(2)], axis=0))
        along_y = from_left(left_ref, jnp.concatenate(columns, axis=1))
        rows = []
        for k in range(2):
            part = along_y[:, k * LANES:(k + 1) * LANES]
            rows.append(jnp.concatenate([part[:size], part[size:]], axis=1))
        potential = from_right(jnp.concatenate(rows, axis=0), right_ref)
        for k in range(2):
            x = first + k
            v0 = potential[k * size:(k + 1) * size, :LANES] * s0
            v1 = potential[k * size:(k + 1) * size, LANES:] * s1
            u = u_ref[x]
            own_ref[0, x] = -(v0 * u)
            own_ref[1, x] = -(v1 * u)
            back_ref[x] = -(v0 * v_ref[0, x] + v1 * w_ref[0, x])


def add_kernel(plan, more_ref, sum_ref, total_ref):
    total_ref[...] = sum_ref[...] + more_ref[...]


def in_hbm(value):
    return pltpu.with_memory_space_constraint(value, pltpu.HBM)


def params():
    return pltpu.CompilerParams(dimension_semantics=("arbitrary",), vmem_limit_bytes=VMEM_BYTES)


def whole(shape):
    return pl.BlockSpec(shape, lambda *_: (0,) * len(shape))


def part(shape, place):
    return pl.BlockSpec((shape[0], 2) + shape[2:], lambda *_: (0, place, 0, 0, 0))


def orbital_block(shape, number, field):
    return pl.BlockSpec((1,) + shape[1:], lambda i, plan: (plan[number * ENTRY + field], 0, 0, 0))


def forward(number, width, plan, u, orbitals, right, left):
    planes, size, lanes = u.shape
    blocks = lax.axis_size("grid")
    shape = (blocks, 2 * width, planes, size // blocks, lanes)
    return pl.pallas_call(
        lambda *refs: forward_kernel(number, *refs),
        grid_spec=pltpu.PrefetchScalarGridSpec(
            num_scalar_prefetch=1,
            grid=(1,),
            in_specs=[
                whole(u.shape),
                orbital_block(orbitals.shape, number, 0),
                orbital_block(orbitals.shape, number, 1),
                whole(right.shape),
                whole(left.shape),
            ],
            out_specs=part(shape, 0),
        ),
        out_shape=pltpu.HBM(shape, jnp.float32),
        cost_estimate=EARLY if number else None,
        compiler_params=params(),
        name="forward_planes",
    )(plan, u, orbitals, orbitals, right, left)


def solve(arrived, kernel, left, right, ahead=None):
    hbm = pl.BlockSpec(memory_space=pl.ANY)
    operands = [in_hbm(arrived), kernel, left, right]
    specs = [part(arrived.shape, 0), whole(kernel.shape), whole(left.shape), whole(right.shape)]
    if ahead is None:
        shape, place, aliases = (arrived.shape[0], 2) + arrived.shape[2:], 0, {}
    else:
        shape, place, aliases = ahead.shape, 1, {len(operands): 0}
        operands.append(in_hbm(ahead))
        specs.append(hbm)
    return pl.pallas_call(
        solve_kernel,
        grid=(1,),
        in_specs=specs,
        out_specs=part(shape, place),
        out_shape=pltpu.HBM(shape, jnp.float32),
        input_output_aliases=aliases,
        compiler_params=params(),
        name="solve_columns",
    )(*operands)


def inverse(number, place, plan, arrived, u, orbitals, left, right):
    own = (2,) + u.shape
    return pl.pallas_call(
        lambda *refs: inverse_kernel(number, *refs),
        grid_spec=pltpu.PrefetchScalarGridSpec(
            num_scalar_prefetch=1,
            grid=(1,),
            in_specs=[
                part(arrived.shape, place),
                whole(u.shape),
                orbital_block(orbitals.shape, number, 0),
                orbital_block(orbitals.shape, number, 1),
                whole(left.shape),
                whole(right.shape),
            ],
            out_specs=[whole(own), whole(u.shape)],
        ),
        out_shape=[pltpu.HBM(own, jnp.float32), pltpu.HBM(u.shape, jnp.float32)],
        compiler_params=params(),
        name="inverse_planes",
    )(plan, in_hbm(arrived), u, orbitals, orbitals, left, right)


def add_into(number, field, plan, total, more):
    count = more.shape[0]
    one = (1,) + more.shape[1:]
    target = pl.BlockSpec(one, lambda i, plan: (plan[number * ENTRY + field + i], 0, 0, 0))
    return pl.pallas_call(
        add_kernel,
        grid_spec=pltpu.PrefetchScalarGridSpec(
            num_scalar_prefetch=1,
            grid=(count,),
            in_specs=[pl.BlockSpec(one, lambda i, plan: (i, 0, 0, 0)), target],
            out_specs=target,
        ),
        out_shape=jax.ShapeDtypeStruct(total.shape, jnp.float32),
        input_output_aliases={2: 0},
        compiler_params=params(),
        name="add_terms",
    )(plan, more, total)


def signed(number, length):
    return jnp.where(number < length // 2, number, number - length)


def coulomb_block(size, column_count, first_column):
    strength = math.sqrt(size**3) / 4.0
    along_x = signed(jnp.arange(size, dtype=jnp.int32), size)
    along_y = signed(first_column + jnp.arange(column_count, dtype=jnp.int32), size)
    squared = along_y[:, None, None] ** 2 + along_x[None, :, None] ** 2 + along_x[None, None, :] ** 2
    bounded = jnp.maximum(squared, 1).astype(jnp.float32)
    kernel = jnp.where(squared == 0, jnp.float32(0.0), jnp.float32(strength) / bounded)
    return kernel * jnp.float32(1.0 / size**3)


def exchange(field):
    return lax.all_to_all(field, "grid", split_axis=0, concat_axis=0, tiled=True)


def to_partner(value):
    pairs = [(g, g ^ (1 << PARTNER_BIT)) for g in range(lax.axis_size("band"))]
    return lax.ppermute(value, "band", pairs)


def sent_orbital(number, plan, orbitals):
    return lax.dynamic_index_in_dim(orbitals, plan[number * ENTRY + 4], 0, keepdims=False)


def one_round(number, plan, orbitals, kernel, total, tables):
    plus, plus_x, minus, minus_x = tables
    u = to_partner(sent_orbital(number, plan, orbitals))
    arrived = exchange(forward(number, 1, plan, u, orbitals, minus, plus))
    arrived = exchange(solve(arrived, kernel, plus_x, minus_x))
    own, back = inverse(number, 0, plan, arrived, u, orbitals, minus, plus)
    total = add_into(number, 0, plan, total, own)
    return add_into(number, 4, plan, total, to_partner(back)[None])


def shards(orbitals, spin_channel):
    count, planes, size, lanes = orbitals.shape
    column_count = size // lax.axis_size("grid")
    plan, sent = make_plan(spin_channel, orbitals)
    us = [to_partner(sent)]
    kernel = coulomb_block(size, column_count, lax.axis_index("grid") * column_count)
    tables = tuple(two_parts(t) for t in fourier_tables(size, planes))
    plus, plus_x, minus, minus_x = tables
    total = lax.cond(
        needs_more(spin_channel),
        lambda *args: one_round(ROUNDS, *args, jnp.zeros_like(orbitals), tables),
        lambda *args: jnp.zeros_like(orbitals),
        plan, orbitals, kernel,
    )
    for number in range(1, ROUNDS):
        sent, us[-1] = lax.optimization_barrier((sent_orbital(number, plan, orbitals), us[-1]))
        us.append(to_partner(sent))

    def planes_of(number):
        return forward(number, 1 if number == 0 else 2, plan, us[number], orbitals, minus, plus)

    returned = []
    arrived = exchange(planes_of(0))
    for number in range(ROUNDS):
        ahead = planes_of(number + 1) if number + 1 < ROUNDS else None
        leaving = solve(arrived, kernel, plus_x, minus_x, ahead)
        if number > 1:
            leaving, returned[number - 2] = lax.optimization_barrier((leaving, returned[number - 2]))
        arrived = exchange(leaving)
        own, back = inverse(number, 0 if ahead is None else 1, plan, arrived, us[number], orbitals, minus, plus)
        returned.append(to_partner(back))
        total = add_into(number, 0, plan, total, own)
        if number > 0:
            total = add_into(number - 1, 4, plan, total, returned[number - 1][None])
    place = plan[(ROUNDS - 1) * ENTRY + 4]
    last = lax.dynamic_index_in_dim(total, place, 0, keepdims=False) + returned[-1]
    return lax.dynamic_update_index_in_dim(total, last, place, 0)


def solution(mesh):
    return jax.shard_map(
        shards,
        mesh=mesh,
        in_specs=(P("band", "grid", None, None), P()),
        out_specs=P("band", "grid", None, None),
        check_vma=False,
    )
```

```python
import math

import jax
import jax.numpy as jnp
import numpy as np
from jax import lax
from jax.experimental import pallas as pl
from jax.experimental.pallas import tpu as pltpu
from jax.sharding import PartitionSpec as P

PARTNER_BIT = 2
ORBITALS = 4
LANES = 128
VMEM_BYTES = 40 * 2**20
EARLY = pl.CostEstimate(flops=10**11, bytes_accessed=200 * 10**6, transcendentals=0)
ROUNDS = 3
ENTRY = 8


def cover(rows, columns, rounds):
    cells = [
        (i, j) for i in range(ORBITALS) for j in range(ORBITALS) if (i < rows) == (j < columns)
    ]

    def search(left, first, second):
        if not left:
            return first, second
        i, j = left[0]
        below = [r for r, c in left if c == j and r != i]
        beside = [c for r, c in left if r == i and c != j]
        options = [(0, r) for r in below] + [(1, c) for c in beside] + [(0, None), (1, None)]
        for side, other in options:
            if len((first, second)[side]) == rounds:
                continue
            taken = {(i, j)}
            if other is not None:
                taken.add((other, j) if side == 0 else (i, other))
            own, far = (i, j) if side == 0 else (j, i)
            entry = (far, own, (own + 1) % ORBITALS if other is None else other, int(other is not None))
            rest = [c for c in left if c not in taken]
            found = search(
                rest,
                first + [entry] if side == 0 else first,
                second + [entry] if side == 1 else second,
            )
            if found is not None:
                return found
        return None

    return search(cells, [], [])


def plan_table():
    patterns = 2**ORBITALS
    bits = [[(p >> i) & 1 for i in range(ORBITALS)] for p in range(patterns)]
    order = [sorted(range(ORBITALS), key=lambda i: b[i]) for b in bits]
    zeros = [b.count(0) for b in bits]
    found = {}
    for rows in range(ORBITALS + 1):
        for columns in range(ORBITALS + 1):
            found[rows, columns] = cover(rows, columns, ROUNDS) or cover(rows, columns, ROUNDS + 1)
    table = np.zeros((2, patterns, patterns, ROUNDS + 1, ENTRY), np.int32)
    table[..., 1] = 1
    for side in range(2):
        for own in range(patterns):
            for other in range(patterns):
                first, second = (own, other) if side == 0 else (other, own)
                both = found[zeros[first], zeros[second]]
                for number, (_, a, b, mask) in enumerate(both[side]):
                    table[side, own, other, number, :4] = (order[own][a], order[own][b], 1, mask)
                for number, (u, *_) in enumerate(both[1 - side]):
                    table[side, own, other, number, 4] = order[own][u]
    rows = np.zeros((2 * patterns * patterns, 1, LANES), np.int32)
    rows[:, 0, :(ROUNDS + 1) * ENTRY] = table.reshape(2 * patterns * patterns, -1)
    return rows


def plan_kernel(spin, table_ref, orbitals_ref, plan_ref, sent_ref, row_ref, sems):
    band = lax.axis_index("band")
    partner = band ^ (1 << PARTNER_BIT)
    row = (band >> PARTNER_BIT) & 1
    for group in (band, partner):
        own = jnp.int32(0)
        for i in range(ORBITALS):
            own = own + spin[group * ORBITALS + i] * (1 << i)
        row = row * 2**ORBITALS + own
    copy = pltpu.make_async_copy(table_ref.at[row], row_ref, sems.at[0])
    copy.start()
    copy.wait()
    copy = pltpu.make_async_copy(orbitals_ref.at[row_ref[0, 4]], sent_ref, sems.at[1])
    copy.start()
    for i in range((ROUNDS + 1) * ENTRY):
        plan_ref[i] = row_ref[0, i]
    copy.wait()


def make_plan(spin_channel, orbitals):
    smem = pl.BlockSpec(memory_space=pltpu.SMEM)
    hbm = pl.BlockSpec(memory_space=pl.ANY)
    return pl.pallas_call(
        plan_kernel,
        in_specs=[smem, hbm, hbm],
        out_specs=[smem, pl.BlockSpec(memory_space=pltpu.VMEM)],
        out_shape=[
            jax.ShapeDtypeStruct(((ROUNDS + 1) * ENTRY,), jnp.int32),
            jax.ShapeDtypeStruct(orbitals.shape[1:], jnp.float32),
        ],
        scratch_shapes=[pltpu.SMEM((1, LANES), jnp.int32), pltpu.SemaphoreType.DMA((2,))],
        name="plan_rounds",
    )(spin_channel, jnp.asarray(plan_table()), orbitals)


def needs_more(spin_channel):
    flip = 1 << PARTNER_BIT
    ones = jnp.sum(spin_channel.reshape(-1, 2, flip, ORBITALS), axis=(1, 3))
    return jnp.any((ones == 0) | (ones == 2 * ORBITALS))


def fourier_tables(length, planes):
    number = np.arange(length)
    angles = (number[:, None] * number[None, :] % length) * (2.0 * math.pi / length)
    cosine, sine = np.cos(angles), np.sin(angles)
    plus = np.block([[cosine, -sine], [sine, cosine]])
    minus = plus.T
    blocks = length // planes
    order = np.arange(2 * length).reshape(2, blocks, planes).transpose(1, 0, 2).reshape(-1)
    return plus, plus[:, order], minus, minus[order, :]


def two_parts(table):
    exact = table.astype(np.float32)
    high = exact.astype(jnp.bfloat16)
    low = (exact - high.astype(np.float32)).astype(jnp.bfloat16)
    return jnp.asarray(np.stack([high, low]))


def split(value):
    high = value.astype(jnp.bfloat16)
    return high, (value - high.astype(jnp.float32)).astype(jnp.bfloat16)


def dot(a, b):
    return jnp.dot(a, b, preferred_element_type=jnp.float32)


def from_left(table_ref, value):
    high, low = split(value)
    return dot(table_ref[0], high) + dot(table_ref[0], low) + dot(table_ref[1], high)


def from_right(value, table_ref):
    high, low = split(value)
    return dot(high, table_ref[0]) + dot(low, table_ref[0]) + dot(high, table_ref[1])


def forward_kernel(number, plan, u_ref, v_ref, w_ref, right_ref, left_ref, out_ref):
    planes, size = u_ref.shape[:2]
    blocks = out_ref.shape[0]
    s0 = plan[number * ENTRY + 2].astype(jnp.float32)
    s1 = plan[number * ENTRY + 3].astype(jnp.float32)
    for first in range(0, planes, 2):
        rows = []
        for x in range(first, first + 2):
            u = u_ref[x]
            rows.append(jnp.concatenate([u * v_ref[0, x] * s0, u * w_ref[0, x] * s1], axis=1))
        along_z = from_right(jnp.concatenate(rows, axis=0), right_ref)
        columns = []
        for k in range(2):
            part = along_z[k * size:(k + 1) * size]
            columns.append(jnp.concatenate([part[:, :LANES], part[:, LANES:]], axis=0))
        along_y = from_left(left_ref, jnp.concatenate(columns, axis=1))
        for k in range(2):
            for c in range(2):
                block = along_y[c * size:(c + 1) * size, k * LANES:(k + 1) * LANES]
                out_ref[:, c, first + k] = block.reshape(blocks, size // blocks, LANES)


def solve_kernel(in_ref, kernel_ref, left_ref, right_ref, *rest):
    out_ref = rest[-1]
    columns = kernel_ref.shape[0]
    rows = math.prod(in_ref.shape[:3])
    flat_in = in_ref.reshape(rows * columns, LANES)
    flat_out = out_ref.reshape(rows * columns, LANES)
    for y in range(0, columns, 2):
        value = jnp.concatenate([flat_in[pl.ds(y + k, rows, stride=columns), :] for k in range(2)], axis=1)
        weight = jnp.concatenate([kernel_ref[y], kernel_ref[y + 1]], axis=1)
        spectrum = from_left(left_ref, value) * jnp.concatenate([weight, weight], axis=0)
        solved = from_left(right_ref, spectrum)
        for k in range(2):
            flat_out[pl.ds(y + k, rows, stride=columns), :] = solved[:, k * LANES:(k + 1) * LANES]


def inverse_kernel(number, plan, in_ref, u_ref, v_ref, w_ref, left_ref, right_ref, own_ref, back_ref):
    planes, size = u_ref.shape[:2]
    s0 = plan[number * ENTRY + 2].astype(jnp.float32)
    s1 = plan[number * ENTRY + 3].astype(jnp.float32)
    for first in range(0, planes, 2):
        columns = []
        for x in range(first, first + 2):
            columns.append(jnp.concatenate([in_ref[:, c, x].reshape(size, LANES) for c in range(2)], axis=0))
        along_y = from_left(left_ref, jnp.concatenate(columns, axis=1))
        rows = []
        for k in range(2):
            part = along_y[:, k * LANES:(k + 1) * LANES]
            rows.append(jnp.concatenate([part[:size], part[size:]], axis=1))
        potential = from_right(jnp.concatenate(rows, axis=0), right_ref)
        for k in range(2):
            x = first + k
            v0 = potential[k * size:(k + 1) * size, :LANES] * s0
            v1 = potential[k * size:(k + 1) * size, LANES:] * s1
            u = u_ref[x]
            own_ref[0, x] = -(v0 * u)
            own_ref[1, x] = -(v1 * u)
            back_ref[x] = -(v0 * v_ref[0, x] + v1 * w_ref[0, x])


def add_kernel(plan, more_ref, sum_ref, total_ref):
    total_ref[...] = sum_ref[...] + more_ref[...]


def in_hbm(value):
    return pltpu.with_memory_space_constraint(value, pltpu.HBM)


def params():
    return pltpu.CompilerParams(dimension_semantics=("arbitrary",), vmem_limit_bytes=VMEM_BYTES)


def whole(shape):
    return pl.BlockSpec(shape, lambda *_: (0,) * len(shape))


def part(shape, place):
    return pl.BlockSpec((shape[0], 2) + shape[2:], lambda *_: (0, place, 0, 0, 0))


def orbital_block(shape, number, field):
    return pl.BlockSpec((1,) + shape[1:], lambda i, plan: (plan[number * ENTRY + field], 0, 0, 0))


def forward(number, width, plan, u, orbitals, right, left):
    planes, size, lanes = u.shape
    blocks = lax.axis_size("grid")
    shape = (blocks, 2 * width, planes, size // blocks, lanes)
    return pl.pallas_call(
        lambda *refs: forward_kernel(number, *refs),
        grid_spec=pltpu.PrefetchScalarGridSpec(
            num_scalar_prefetch=1,
            grid=(1,),
            in_specs=[
                whole(u.shape),
                orbital_block(orbitals.shape, number, 0),
                orbital_block(orbitals.shape, number, 1),
                whole(right.shape),
                whole(left.shape),
            ],
            out_specs=part(shape, 0),
        ),
        out_shape=pltpu.HBM(shape, jnp.float32),
        cost_estimate=EARLY if number else None,
        compiler_params=params(),
        name="forward_planes",
    )(plan, u, orbitals, orbitals, right, left)


def solve(arrived, kernel, left, right, ahead=None):
    hbm = pl.BlockSpec(memory_space=pl.ANY)
    operands = [in_hbm(arrived), kernel, left, right]
    specs = [part(arrived.shape, 0), whole(kernel.shape), whole(left.shape), whole(right.shape)]
    if ahead is None:
        shape, place, aliases = (arrived.shape[0], 2) + arrived.shape[2:], 0, {}
    else:
        shape, place, aliases = ahead.shape, 1, {len(operands): 0}
        operands.append(in_hbm(ahead))
        specs.append(hbm)
    return pl.pallas_call(
        solve_kernel,
        grid=(1,),
        in_specs=specs,
        out_specs=part(shape, place),
        out_shape=pltpu.HBM(shape, jnp.float32),
        input_output_aliases=aliases,
        compiler_params=params(),
        name="solve_columns",
    )(*operands)


def inverse(number, place, plan, arrived, u, orbitals, left, right):
    own = (2,) + u.shape
    return pl.pallas_call(
        lambda *refs: inverse_kernel(number, *refs),
        grid_spec=pltpu.PrefetchScalarGridSpec(
            num_scalar_prefetch=1,
            grid=(1,),
            in_specs=[
                part(arrived.shape, place),
                whole(u.shape),
                orbital_block(orbitals.shape, number, 0),
                orbital_block(orbitals.shape, number, 1),
                whole(left.shape),
                whole(right.shape),
            ],
            out_specs=[whole(own), whole(u.shape)],
        ),
        out_shape=[pltpu.HBM(own, jnp.float32), pltpu.HBM(u.shape, jnp.float32)],
        compiler_params=params(),
        name="inverse_planes",
    )(plan, in_hbm(arrived), u, orbitals, orbitals, left, right)


def add_into(number, field, plan, total, more):
    count = more.shape[0]
    one = (1,) + more.shape[1:]
    target = pl.BlockSpec(one, lambda i, plan: (plan[number * ENTRY + field + i], 0, 0, 0))
    return pl.pallas_call(
        add_kernel,
        grid_spec=pltpu.PrefetchScalarGridSpec(
            num_scalar_prefetch=1,
            grid=(count,),
            in_specs=[pl.BlockSpec(one, lambda i, plan: (i, 0, 0, 0)), target],
            out_specs=target,
        ),
        out_shape=jax.ShapeDtypeStruct(total.shape, jnp.float32),
        input_output_aliases={2: 0},
        compiler_params=params(),
        name="add_terms",
    )(plan, more, total)


def signed(number, length):
    return jnp.where(number < length // 2, number, number - length)


def coulomb_block(size, column_count, first_column):
    strength = math.sqrt(size**3) / 4.0
    along_x = signed(jnp.arange(size, dtype=jnp.int32), size)
    along_y = signed(first_column + jnp.arange(column_count, dtype=jnp.int32), size)
    squared = along_y[:, None, None] ** 2 + along_x[None, :, None] ** 2 + along_x[None, None, :] ** 2
    bounded = jnp.maximum(squared, 1).astype(jnp.float32)
    kernel = jnp.where(squared == 0, jnp.float32(0.0), jnp.float32(strength) / bounded)
    return kernel * jnp.float32(1.0 / size**3)


def exchange(field):
    return lax.all_to_all(field, "grid", split_axis=0, concat_axis=0, tiled=True)


def to_partner(value):
    pairs = [(g, g ^ (1 << PARTNER_BIT)) for g in range(lax.axis_size("band"))]
    return lax.ppermute(value, "band", pairs)


def sent_orbital(number, plan, orbitals):
    return lax.dynamic_index_in_dim(orbitals, plan[number * ENTRY + 4], 0, keepdims=False)


def in_rounds(rounds, plan, received, orbitals, kernel, sends, tables):
    plus, plus_x, minus, minus_x = tables
    us = [received]
    for number in range(1, rounds):
        sent, us[-1] = lax.optimization_barrier((sends[number - 1], us[-1]))
        us.append(to_partner(sent))

    def planes_of(number):
        return forward(number, 1 if number == 0 else 2, plan, us[number], orbitals, minus, plus)

    total = jnp.zeros_like(orbitals)
    returned = []
    arrived = exchange(planes_of(0))
    for number in range(rounds):
        ahead = planes_of(number + 1) if number + 1 < rounds else None
        leaving = solve(arrived, kernel, plus_x, minus_x, ahead)
        if number > 1:
            leaving, returned[number - 2] = lax.optimization_barrier((leaving, returned[number - 2]))
        arrived = exchange(leaving)
        own, back = inverse(number, 0 if ahead is None else 1, plan, arrived, us[number], orbitals, minus, plus)
        returned.append(to_partner(back))
        total = add_into(number, 0, plan, total, own)
        if number > 0:
            total = add_into(number - 1, 4, plan, total, returned[number - 1][None])
    place = plan[(rounds - 1) * ENTRY + 4]
    last = lax.dynamic_index_in_dim(total, place, 0, keepdims=False) + returned[-1]
    return lax.dynamic_update_index_in_dim(total, last, place, 0)


def shards(orbitals, spin_channel):
    count, planes, size, lanes = orbitals.shape
    column_count = size // lax.axis_size("grid")
    plan, sent = make_plan(spin_channel, orbitals)
    received = to_partner(sent)
    sends = [sent_orbital(number, plan, orbitals) for number in range(1, ROUNDS + 1)]
    kernel = coulomb_block(size, column_count, lax.axis_index("grid") * column_count)
    tables = tuple(two_parts(t) for t in fourier_tables(size, planes))
    more, kernel, sends = lax.optimization_barrier((needs_more(spin_channel), kernel, sends))
    return lax.cond(
        more,
        lambda *args: in_rounds(ROUNDS + 1, *args, tables),
        lambda *args: in_rounds(ROUNDS, *args, tables),
        plan, received, orbitals, kernel, sends,
    )


def solution(mesh):
    return jax.shard_map(
        shards,
        mesh=mesh,
        in_specs=(P("band", "grid", None, None), P()),
        out_specs=P("band", "grid", None, None),
        check_vma=False,
    )
```

```python
import math

import jax
import jax.numpy as jnp
import numpy as np
from jax import lax
from jax.experimental import pallas as pl
from jax.experimental.pallas import tpu as pltpu
from jax.sharding import PartitionSpec as P

PARTNER_BIT = 2
ORBITALS = 4
LANES = 128
VMEM_BYTES = 40 * 2**20
EARLY = pl.CostEstimate(flops=10**11, bytes_accessed=200 * 10**6, transcendentals=0)
ROUNDS = 3
ENTRY = 8


def cover(rows, columns, rounds):
    cells = [
        (i, j) for i in range(ORBITALS) for j in range(ORBITALS) if (i < rows) == (j < columns)
    ]

    def search(left, first, second):
        if not left:
            return first, second
        i, j = left[0]
        below = [r for r, c in left if c == j and r != i]
        beside = [c for r, c in left if r == i and c != j]
        options = [(0, r) for r in below] + [(1, c) for c in beside] + [(0, None), (1, None)]
        for side, other in options:
            if len((first, second)[side]) == rounds:
                continue
            taken = {(i, j)}
            if other is not None:
                taken.add((other, j) if side == 0 else (i, other))
            own, far = (i, j) if side == 0 else (j, i)
            entry = (far, own, (own + 1) % ORBITALS if other is None else other, int(other is not None))
            rest = [c for c in left if c not in taken]
            found = search(
                rest,
                first + [entry] if side == 0 else first,
                second + [entry] if side == 1 else second,
            )
            if found is not None:
                return found
        return None

    return search(cells, [], [])


def plan_table():
    patterns = 2**ORBITALS
    bits = [[(p >> i) & 1 for i in range(ORBITALS)] for p in range(patterns)]
    order = [sorted(range(ORBITALS), key=lambda i: b[i]) for b in bits]
    zeros = [b.count(0) for b in bits]
    found = {}
    for rows in range(ORBITALS + 1):
        for columns in range(ORBITALS + 1):
            found[rows, columns] = cover(rows, columns, ROUNDS) or cover(rows, columns, ROUNDS + 1)
    table = np.zeros((2, patterns, patterns, ROUNDS + 1, ENTRY), np.int32)
    table[..., 1] = 1
    for side in range(2):
        for own in range(patterns):
            for other in range(patterns):
                first, second = (own, other) if side == 0 else (other, own)
                both = found[zeros[first], zeros[second]]
                for number, (_, a, b, mask) in enumerate(both[side]):
                    table[side, own, other, number, :4] = (order[own][a], order[own][b], 1, mask)
                for number, (u, *_) in enumerate(both[1 - side]):
                    table[side, own, other, number, 4] = order[own][u]
    rows = np.zeros((2 * patterns * patterns, 1, LANES), np.int32)
    rows[:, 0, :(ROUNDS + 1) * ENTRY] = table.reshape(2 * patterns * patterns, -1)
    return rows


def plan_kernel(spin, table_ref, orbitals_ref, plan_ref, sent_ref, row_ref, sems):
    band = lax.axis_index("band")
    partner = band ^ (1 << PARTNER_BIT)
    row = (band >> PARTNER_BIT) & 1
    for group in (band, partner):
        own = jnp.int32(0)
        for i in range(ORBITALS):
            own = own + spin[group * ORBITALS + i] * (1 << i)
        row = row * 2**ORBITALS + own
    copy = pltpu.make_async_copy(table_ref.at[row], row_ref, sems.at[0])
    copy.start()
    copy.wait()
    copy = pltpu.make_async_copy(orbitals_ref.at[row_ref[0, 4]], sent_ref, sems.at[1])
    copy.start()
    for i in range((ROUNDS + 1) * ENTRY):
        plan_ref[i] = row_ref[0, i]
    copy.wait()


def make_plan(spin_channel, orbitals):
    smem = pl.BlockSpec(memory_space=pltpu.SMEM)
    hbm = pl.BlockSpec(memory_space=pl.ANY)
    return pl.pallas_call(
        plan_kernel,
        in_specs=[smem, hbm, hbm],
        out_specs=[smem, pl.BlockSpec(memory_space=pltpu.VMEM)],
        out_shape=[
            jax.ShapeDtypeStruct(((ROUNDS + 1) * ENTRY,), jnp.int32),
            jax.ShapeDtypeStruct(orbitals.shape[1:], jnp.float32),
        ],
        scratch_shapes=[pltpu.SMEM((1, LANES), jnp.int32), pltpu.SemaphoreType.DMA((2,))],
        name="plan_rounds",
    )(spin_channel, jnp.asarray(plan_table()), orbitals)


def needs_more(spin_channel):
    flip = 1 << PARTNER_BIT
    ones = jnp.sum(spin_channel.reshape(-1, 2, flip, ORBITALS), axis=(1, 3))
    return jnp.any((ones == 0) | (ones == 2 * ORBITALS))


def fourier_tables(length, planes):
    number = np.arange(length)
    angles = (number[:, None] * number[None, :] % length) * (2.0 * math.pi / length)
    cosine, sine = np.cos(angles), np.sin(angles)
    plus = np.block([[cosine, -sine], [sine, cosine]])
    minus = plus.T
    blocks = length // planes
    order = np.arange(2 * length).reshape(2, blocks, planes).transpose(1, 0, 2).reshape(-1)
    return plus, plus[:, order], minus, minus[order, :]


def two_parts(table):
    exact = table.astype(np.float32)
    high = exact.astype(jnp.bfloat16)
    low = (exact - high.astype(np.float32)).astype(jnp.bfloat16)
    return jnp.asarray(np.stack([high, low]))


def split(value):
    high = value.astype(jnp.bfloat16)
    return high, (value - high.astype(jnp.float32)).astype(jnp.bfloat16)


def dot(a, b):
    return jnp.dot(a, b, preferred_element_type=jnp.float32)


def from_left(table_ref, value):
    high, low = split(value)
    return dot(table_ref[0], high) + dot(table_ref[0], low) + dot(table_ref[1], high)


def from_right(value, table_ref):
    high, low = split(value)
    return dot(high, table_ref[0]) + dot(low, table_ref[0]) + dot(high, table_ref[1])


def forward_kernel(number, plan, u_ref, v_ref, w_ref, right_ref, left_ref, out_ref):
    planes, size = u_ref.shape[:2]
    blocks = out_ref.shape[0]
    s0 = plan[number * ENTRY + 2].astype(jnp.float32)
    s1 = plan[number * ENTRY + 3].astype(jnp.float32)
    for first in range(0, planes, 2):
        rows = []
        for x in range(first, first + 2):
            u = u_ref[x]
            rows.append(jnp.concatenate([u * v_ref[0, x] * s0, u * w_ref[0, x] * s1], axis=1))
        along_z = from_right(jnp.concatenate(rows, axis=0), right_ref)
        columns = []
        for k in range(2):
            part = along_z[k * size:(k + 1) * size]
            columns.append(jnp.concatenate([part[:, :LANES], part[:, LANES:]], axis=0))
        along_y = from_left(left_ref, jnp.concatenate(columns, axis=1))
        for k in range(2):
            for c in range(2):
                block = along_y[c * size:(c + 1) * size, k * LANES:(k + 1) * LANES]
                out_ref[:, c, first + k] = block.reshape(blocks, size // blocks, LANES)


def solve_kernel(in_ref, kernel_ref, left_ref, right_ref, *rest):
    out_ref = rest[-1]
    columns = kernel_ref.shape[0]
    rows = math.prod(in_ref.shape[:3])
    flat_in = in_ref.reshape(rows * columns, LANES)
    flat_out = out_ref.reshape(rows * columns, LANES)
    for y in range(0, columns, 2):
        value = jnp.concatenate([flat_in[pl.ds(y + k, rows, stride=columns), :] for k in range(2)], axis=1)
        weight = jnp.concatenate([kernel_ref[y], kernel_ref[y + 1]], axis=1)
        spectrum = from_left(left_ref, value) * jnp.concatenate([weight, weight], axis=0)
        solved = from_left(right_ref, spectrum)
        for k in range(2):
            flat_out[pl.ds(y + k, rows, stride=columns), :] = solved[:, k * LANES:(k + 1) * LANES]


def inverse_kernel(number, plan, in_ref, u_ref, v_ref, w_ref, left_ref, right_ref, own_ref, back_ref):
    planes, size = u_ref.shape[:2]
    s0 = plan[number * ENTRY + 2].astype(jnp.float32)
    s1 = plan[number * ENTRY + 3].astype(jnp.float32)
    for first in range(0, planes, 2):
        columns = []
        for x in range(first, first + 2):
            columns.append(jnp.concatenate([in_ref[:, c, x].reshape(size, LANES) for c in range(2)], axis=0))
        along_y = from_left(left_ref, jnp.concatenate(columns, axis=1))
        rows = []
        for k in range(2):
            part = along_y[:, k * LANES:(k + 1) * LANES]
            rows.append(jnp.concatenate([part[:size], part[size:]], axis=1))
        potential = from_right(jnp.concatenate(rows, axis=0), right_ref)
        for k in range(2):
            x = first + k
            v0 = potential[k * size:(k + 1) * size, :LANES] * s0
            v1 = potential[k * size:(k + 1) * size, LANES:] * s1
            u = u_ref[x]
            own_ref[0, x] = -(v0 * u)
            own_ref[1, x] = -(v1 * u)
            back_ref[x] = -(v0 * v_ref[0, x] + v1 * w_ref[0, x])


def solve_and_inverse_kernel(
    number, plan, in_ref, kernel_ref, left_x_ref, right_x_ref, u_ref, v_ref, w_ref, left_ref, right_ref,
    out_ref, own_ref, back_ref,
):
    blocks, parts, planes, columns, lanes = in_ref.shape
    rows = blocks * 2 * planes
    each = 2 * planes
    flat_in = in_ref.reshape(blocks * parts * planes * columns, lanes)
    flat_out = out_ref.reshape(rows * columns, lanes)
    for y in range(0, columns, 2):
        halves = []
        for k in range(2):
            places = [block * parts * planes * columns + y + k for block in range(blocks)]
            halves.append(
                jnp.concatenate([flat_in[pl.ds(place, each, stride=columns), :] for place in places], axis=0)
            )
        weight = jnp.concatenate([kernel_ref[y], kernel_ref[y + 1]], axis=1)
        spectrum = from_left(left_x_ref, jnp.concatenate(halves, axis=1))
        solved = from_left(right_x_ref, spectrum * jnp.concatenate([weight, weight], axis=0))
        for k in range(2):
            flat_out[pl.ds(y + k, rows, stride=columns), :] = solved[:, k * lanes:(k + 1) * lanes]
    inverse_kernel(
        number, plan, in_ref.at[:, pl.ds(2, 2)], u_ref, v_ref, w_ref, left_ref, right_ref, own_ref, back_ref
    )


def add_kernel(plan, more_ref, sum_ref, total_ref):
    total_ref[...] = sum_ref[...] + more_ref[...]


def in_hbm(value):
    return pltpu.with_memory_space_constraint(value, pltpu.HBM)


def params():
    return pltpu.CompilerParams(dimension_semantics=("arbitrary",), vmem_limit_bytes=VMEM_BYTES)


def whole(shape):
    return pl.BlockSpec(shape, lambda *_: (0,) * len(shape))


def part(shape, place):
    return pl.BlockSpec((shape[0], 2) + shape[2:], lambda *_: (0, place, 0, 0, 0))


def orbital_block(shape, number, field):
    return pl.BlockSpec((1,) + shape[1:], lambda i, plan: (plan[number * ENTRY + field], 0, 0, 0))


def forward(number, width, plan, u, orbitals, right, left):
    planes, size, lanes = u.shape
    blocks = lax.axis_size("grid")
    shape = (blocks, 2 * width, planes, size // blocks, lanes)
    return pl.pallas_call(
        lambda *refs: forward_kernel(number, *refs),
        grid_spec=pltpu.PrefetchScalarGridSpec(
            num_scalar_prefetch=1,
            grid=(1,),
            in_specs=[
                whole(u.shape),
                orbital_block(orbitals.shape, number, 0),
                orbital_block(orbitals.shape, number, 1),
                whole(right.shape),
                whole(left.shape),
            ],
            out_specs=part(shape, 0),
        ),
        out_shape=pltpu.HBM(shape, jnp.float32),
        cost_estimate=EARLY if number else None,
        compiler_params=params(),
        name="forward_planes",
    )(plan, u, orbitals, orbitals, right, left)


def solve(arrived, kernel, left, right, ahead=None):
    hbm = pl.BlockSpec(memory_space=pl.ANY)
    operands = [in_hbm(arrived), kernel, left, right]
    specs = [part(arrived.shape, 0), whole(kernel.shape), whole(left.shape), whole(right.shape)]
    if ahead is None:
        shape, place, aliases = (arrived.shape[0], 2) + arrived.shape[2:], 0, {}
    else:
        shape, place, aliases = ahead.shape, 1, {len(operands): 0}
        operands.append(in_hbm(ahead))
        specs.append(hbm)
    return pl.pallas_call(
        solve_kernel,
        grid=(1,),
        in_specs=specs,
        out_specs=part(shape, place),
        out_shape=pltpu.HBM(shape, jnp.float32),
        input_output_aliases=aliases,
        compiler_params=params(),
        name="solve_columns",
    )(*operands)


def inverse(number, place, plan, arrived, u, orbitals, left, right):
    own = (2,) + u.shape
    return pl.pallas_call(
        lambda *refs: inverse_kernel(number, *refs),
        grid_spec=pltpu.PrefetchScalarGridSpec(
            num_scalar_prefetch=1,
            grid=(1,),
            in_specs=[
                part(arrived.shape, place),
                whole(u.shape),
                orbital_block(orbitals.shape, number, 0),
                orbital_block(orbitals.shape, number, 1),
                whole(left.shape),
                whole(right.shape),
            ],
            out_specs=[whole(own), whole(u.shape)],
        ),
        out_shape=[pltpu.HBM(own, jnp.float32), pltpu.HBM(u.shape, jnp.float32)],
        compiler_params=params(),
        name="inverse_planes",
    )(plan, in_hbm(arrived), u, orbitals, orbitals, left, right)


def solve_and_inverse(number, plan, arrived, kernel, left_x, right_x, u, orbitals, left, right):
    own = (2,) + u.shape
    field = (arrived.shape[0], 2) + arrived.shape[2:]
    return pl.pallas_call(
        lambda *refs: solve_and_inverse_kernel(number, *refs),
        grid_spec=pltpu.PrefetchScalarGridSpec(
            num_scalar_prefetch=1,
            grid=(1,),
            in_specs=[
                whole(arrived.shape),
                whole(kernel.shape),
                whole(left_x.shape),
                whole(right_x.shape),
                whole(u.shape),
                orbital_block(orbitals.shape, number, 0),
                orbital_block(orbitals.shape, number, 1),
                whole(left.shape),
                whole(right.shape),
            ],
            out_specs=[whole(field), whole(own), whole(u.shape)],
        ),
        out_shape=[
            pltpu.HBM(field, jnp.float32), pltpu.HBM(own, jnp.float32), pltpu.HBM(u.shape, jnp.float32)
        ],
        compiler_params=params(),
        name="solve_and_inverse",
    )(plan, in_hbm(arrived), kernel, left_x, right_x, u, orbitals, orbitals, left, right)


def add_into(number, field, plan, total, more):
    count = more.shape[0]
    one = (1,) + more.shape[1:]
    target = pl.BlockSpec(one, lambda i, plan: (plan[number * ENTRY + field + i], 0, 0, 0))
    return pl.pallas_call(
        add_kernel,
        grid_spec=pltpu.PrefetchScalarGridSpec(
            num_scalar_prefetch=1,
            grid=(count,),
            in_specs=[pl.BlockSpec(one, lambda i, plan: (i, 0, 0, 0)), target],
            out_specs=target,
        ),
        out_shape=jax.ShapeDtypeStruct(total.shape, jnp.float32),
        input_output_aliases={2: 0},
        compiler_params=params(),
        name="add_terms",
    )(plan, more, total)


def signed(number, length):
    return jnp.where(number < length // 2, number, number - length)


def coulomb_block(size, column_count, first_column):
    strength = math.sqrt(size**3) / 4.0
    along_x = signed(jnp.arange(size, dtype=jnp.int32), size)
    along_y = signed(first_column + jnp.arange(column_count, dtype=jnp.int32), size)
    squared = along_y[:, None, None] ** 2 + along_x[None, :, None] ** 2 + along_x[None, None, :] ** 2
    bounded = jnp.maximum(squared, 1).astype(jnp.float32)
    kernel = jnp.where(squared == 0, jnp.float32(0.0), jnp.float32(strength) / bounded)
    return kernel * jnp.float32(1.0 / size**3)


def exchange(field):
    return lax.all_to_all(field, "grid", split_axis=0, concat_axis=0, tiled=True)


def to_partner(value):
    pairs = [(g, g ^ (1 << PARTNER_BIT)) for g in range(lax.axis_size("band"))]
    return lax.ppermute(value, "band", pairs)


def sent_orbital(number, plan, orbitals):
    return lax.dynamic_index_in_dim(orbitals, plan[number * ENTRY + 4], 0, keepdims=False)


def in_rounds(rounds, plan, received, orbitals, kernel, sends, tables):
    plus, plus_x, minus, minus_x = tables
    us = [received]
    for number in range(1, rounds):
        sent, us[-1] = lax.optimization_barrier((sends[number - 1], us[-1]))
        us.append(to_partner(sent))

    def planes_of(number):
        return forward(number, 1 if number == 0 else 2, plan, us[number], orbitals, minus, plus)

    total = jnp.zeros_like(orbitals)
    returned, owns = [], []

    def give(own, back):
        owns.append(own)
        returned.append(to_partner(back))

    arrived = exchange(planes_of(0))
    for number in range(rounds - 1):
        leaving = solve(arrived, kernel, plus_x, minus_x, planes_of(number + 1))
        if number > 1:
            leaving, returned[number - 2] = lax.optimization_barrier((leaving, returned[number - 2]))
        arrived = exchange(leaving)
        if number < rounds - 2:
            give(*inverse(number, 1, plan, arrived, us[number], orbitals, minus, plus))
    leaving, own, back = solve_and_inverse(
        rounds - 2, plan, arrived, kernel, plus_x, minus_x, us[rounds - 2], orbitals, minus, plus
    )
    leaving, returned[rounds - 3] = lax.optimization_barrier((leaving, returned[rounds - 3]))
    arrived = exchange(leaving)
    give(own, back)
    give(*inverse(rounds - 1, 0, plan, arrived, us[rounds - 1], orbitals, minus, plus))
    for number in range(rounds):
        total = add_into(number, 0, plan, total, owns[number])
        if number > 0:
            total = add_into(number - 1, 4, plan, total, returned[number - 1][None])
    place = plan[(rounds - 1) * ENTRY + 4]
    last = lax.dynamic_index_in_dim(total, place, 0, keepdims=False) + returned[-1]
    return lax.dynamic_update_index_in_dim(total, last, place, 0)


def shards(orbitals, spin_channel):
    count, planes, size, lanes = orbitals.shape
    column_count = size // lax.axis_size("grid")
    plan, sent = make_plan(spin_channel, orbitals)
    received = to_partner(sent)
    sends = [sent_orbital(number, plan, orbitals) for number in range(1, ROUNDS + 1)]
    kernel = coulomb_block(size, column_count, lax.axis_index("grid") * column_count)
    tables = tuple(two_parts(t) for t in fourier_tables(size, planes))
    more, kernel, sends = lax.optimization_barrier((needs_more(spin_channel), kernel, sends))
    return lax.cond(
        more,
        lambda *args: in_rounds(ROUNDS + 1, *args, tables),
        lambda *args: in_rounds(ROUNDS, *args, tables),
        plan, received, orbitals, kernel, sends,
    )


def solution(mesh):
    return jax.shard_map(
        shards,
        mesh=mesh,
        in_specs=(P("band", "grid", None, None), P()),
        out_specs=P("band", "grid", None, None),
        check_vma=False,
    )
```

```python
import math

import jax
import jax.numpy as jnp
import numpy as np
from jax import lax
from jax.experimental import pallas as pl
from jax.experimental.pallas import tpu as pltpu
from jax.sharding import PartitionSpec as P

PARTNER_BIT = 2
ORBITALS = 4
LANES = 128
VMEM_BYTES = 40 * 2**20
EARLY = pl.CostEstimate(flops=10**11, bytes_accessed=200 * 10**6, transcendentals=0)
ROUNDS = 3
ENTRY = 8


def cover(rows, columns, rounds):
    cells = [
        (i, j) for i in range(ORBITALS) for j in range(ORBITALS) if (i < rows) == (j < columns)
    ]

    def search(left, first, second):
        if not left:
            return first, second
        i, j = left[0]
        below = [r for r, c in left if c == j and r != i]
        beside = [c for r, c in left if r == i and c != j]
        options = [(0, r) for r in below] + [(1, c) for c in beside] + [(0, None), (1, None)]
        for side, other in options:
            if len((first, second)[side]) == rounds:
                continue
            taken = {(i, j)}
            if other is not None:
                taken.add((other, j) if side == 0 else (i, other))
            own, far = (i, j) if side == 0 else (j, i)
            entry = (far, own, (own + 1) % ORBITALS if other is None else other, int(other is not None))
            rest = [c for c in left if c not in taken]
            found = search(
                rest,
                first + [entry] if side == 0 else first,
                second + [entry] if side == 1 else second,
            )
            if found is not None:
                return found
        return None

    return search(cells, [], [])


def plan_table():
    patterns = 2**ORBITALS
    bits = [[(p >> i) & 1 for i in range(ORBITALS)] for p in range(patterns)]
    order = [sorted(range(ORBITALS), key=lambda i: b[i]) for b in bits]
    zeros = [b.count(0) for b in bits]
    found = {}
    for rows in range(ORBITALS + 1):
        for columns in range(ORBITALS + 1):
            found[rows, columns] = cover(rows, columns, ROUNDS) or cover(rows, columns, ROUNDS + 1)
    table = np.zeros((2, patterns, patterns, ROUNDS + 1, ENTRY), np.int32)
    table[..., 1] = 1
    for side in range(2):
        for own in range(patterns):
            for other in range(patterns):
                first, second = (own, other) if side == 0 else (other, own)
                both = found[zeros[first], zeros[second]]
                for number, (_, a, b, mask) in enumerate(both[side]):
                    table[side, own, other, number, :4] = (order[own][a], order[own][b], 1, mask)
                for number, (u, *_) in enumerate(both[1 - side]):
                    table[side, own, other, number, 4] = order[own][u]
    rows = np.zeros((2 * patterns * patterns, 1, LANES), np.int32)
    rows[:, 0, :(ROUNDS + 1) * ENTRY] = table.reshape(2 * patterns * patterns, -1)
    return rows


def plan_kernel(spin, table_ref, orbitals_ref, plan_ref, sent_ref, row_ref, sems):
    band = lax.axis_index("band")
    partner = band ^ (1 << PARTNER_BIT)
    row = (band >> PARTNER_BIT) & 1
    for group in (band, partner):
        own = jnp.int32(0)
        for i in range(ORBITALS):
            own = own + spin[group * ORBITALS + i] * (1 << i)
        row = row * 2**ORBITALS + own
    copy = pltpu.make_async_copy(table_ref.at[row], row_ref, sems.at[0])
    copy.start()
    copy.wait()
    copy = pltpu.make_async_copy(orbitals_ref.at[row_ref[0, 4]], sent_ref, sems.at[1])
    copy.start()
    for i in range((ROUNDS + 1) * ENTRY):
        plan_ref[i] = row_ref[0, i]
    copy.wait()


def make_plan(spin_channel, orbitals):
    smem = pl.BlockSpec(memory_space=pltpu.SMEM)
    hbm = pl.BlockSpec(memory_space=pl.ANY)
    return pl.pallas_call(
        plan_kernel,
        in_specs=[smem, hbm, hbm],
        out_specs=[smem, pl.BlockSpec(memory_space=pltpu.VMEM)],
        out_shape=[
            jax.ShapeDtypeStruct(((ROUNDS + 1) * ENTRY,), jnp.int32),
            jax.ShapeDtypeStruct(orbitals.shape[1:], jnp.float32),
        ],
        scratch_shapes=[pltpu.SMEM((1, LANES), jnp.int32), pltpu.SemaphoreType.DMA((2,))],
        name="plan_rounds",
    )(spin_channel, jnp.asarray(plan_table()), orbitals)


def needs_more(spin_channel):
    flip = 1 << PARTNER_BIT
    ones = jnp.sum(spin_channel.reshape(-1, 2, flip, ORBITALS), axis=(1, 3))
    return jnp.any((ones == 0) | (ones == 2 * ORBITALS))


def fourier_tables(length, planes):
    number = np.arange(length)
    angles = (number[:, None] * number[None, :] % length) * (2.0 * math.pi / length)
    cosine, sine = np.cos(angles), np.sin(angles)
    plus = np.block([[cosine, -sine], [sine, cosine]])
    minus = plus.T
    blocks = length // planes
    order = np.arange(2 * length).reshape(2, blocks, planes).transpose(1, 0, 2).reshape(-1)
    return plus, plus[:, order], minus, minus[order, :]


def two_parts(table):
    exact = table.astype(np.float32)
    high = exact.astype(jnp.bfloat16)
    low = (exact - high.astype(np.float32)).astype(jnp.bfloat16)
    return jnp.asarray(np.stack([high, low]))


def split(value):
    high = value.astype(jnp.bfloat16)
    return high, (value - high.astype(jnp.float32)).astype(jnp.bfloat16)


def dot(a, b):
    return jnp.dot(a, b, preferred_element_type=jnp.float32)


def from_left(table_ref, value):
    high, low = split(value)
    return dot(table_ref[0], high) + dot(table_ref[0], low) + dot(table_ref[1], high)


def from_right(value, table_ref):
    high, low = split(value)
    return dot(high, table_ref[0]) + dot(low, table_ref[0]) + dot(high, table_ref[1])


def forward_kernel(number, plan, u_ref, v_ref, w_ref, right_ref, left_ref, out_ref):
    planes, size = u_ref.shape[:2]
    blocks = out_ref.shape[0]
    s0 = plan[number * ENTRY + 2].astype(jnp.float32)
    s1 = plan[number * ENTRY + 3].astype(jnp.float32)
    for first in range(0, planes, 2):
        rows = []
        for x in range(first, first + 2):
            u = u_ref[x]
            rows.append(jnp.concatenate([u * v_ref[0, x] * s0, u * w_ref[0, x] * s1], axis=1))
        along_z = from_right(jnp.concatenate(rows, axis=0), right_ref)
        columns = []
        for k in range(2):
            part = along_z[k * size:(k + 1) * size]
            columns.append(jnp.concatenate([part[:, :LANES], part[:, LANES:]], axis=0))
        along_y = from_left(left_ref, jnp.concatenate(columns, axis=1))
        for k in range(2):
            for c in range(2):
                block = along_y[c * size:(c + 1) * size, k * LANES:(k + 1) * LANES]
                out_ref[:, c, first + k] = block.reshape(blocks, size // blocks, LANES)


def solve_kernel(in_ref, kernel_ref, left_ref, right_ref, *rest):
    out_ref = rest[-1]
    columns = kernel_ref.shape[0]
    rows = math.prod(in_ref.shape[:3])
    flat_in = in_ref.reshape(rows * columns, LANES)
    flat_out = out_ref.reshape(rows * columns, LANES)
    for y in range(0, columns, 2):
        value = jnp.concatenate([flat_in[pl.ds(y + k, rows, stride=columns), :] for k in range(2)], axis=1)
        weight = jnp.concatenate([kernel_ref[y], kernel_ref[y + 1]], axis=1)
        spectrum = from_left(left_ref, value) * jnp.concatenate([weight, weight], axis=0)
        solved = from_left(right_ref, spectrum)
        for k in range(2):
            flat_out[pl.ds(y + k, rows, stride=columns), :] = solved[:, k * LANES:(k + 1) * LANES]


def inverse_kernel(number, plan, in_ref, u_ref, v_ref, w_ref, left_ref, right_ref, own_ref, back_ref):
    planes, size = u_ref.shape[:2]
    s0 = plan[number * ENTRY + 2].astype(jnp.float32)
    s1 = plan[number * ENTRY + 3].astype(jnp.float32)
    for first in range(0, planes, 2):
        columns = []
        for x in range(first, first + 2):
            columns.append(jnp.concatenate([in_ref[:, c, x].reshape(size, LANES) for c in range(2)], axis=0))
        along_y = from_left(left_ref, jnp.concatenate(columns, axis=1))
        rows = []
        for k in range(2):
            part = along_y[:, k * LANES:(k + 1) * LANES]
            rows.append(jnp.concatenate([part[:size], part[size:]], axis=1))
        potential = from_right(jnp.concatenate(rows, axis=0), right_ref)
        for k in range(2):
            x = first + k
            v0 = potential[k * size:(k + 1) * size, :LANES] * s0
            v1 = potential[k * size:(k + 1) * size, LANES:] * s1
            u = u_ref[x]
            own_ref[0, x] = -(v0 * u)
            own_ref[1, x] = -(v1 * u)
            back_ref[x] = -(v0 * v_ref[0, x] + v1 * w_ref[0, x])


def solve_and_inverse_kernel(
    number, plan, in_ref, kernel_ref, left_x_ref, right_x_ref, u_ref, v_ref, w_ref, left_ref, right_ref,
    out_ref, own_ref, back_ref,
):
    blocks, parts, planes, columns, lanes = in_ref.shape
    rows = blocks * 2 * planes
    each = 2 * planes
    flat_in = in_ref.reshape(blocks * parts * planes * columns, lanes)
    flat_out = out_ref.reshape(rows * columns, lanes)
    for y in range(0, columns, 2):
        halves = []
        for k in range(2):
            places = [block * parts * planes * columns + y + k for block in range(blocks)]
            halves.append(
                jnp.concatenate([flat_in[pl.ds(place, each, stride=columns), :] for place in places], axis=0)
            )
        weight = jnp.concatenate([kernel_ref[y], kernel_ref[y + 1]], axis=1)
        spectrum = from_left(left_x_ref, jnp.concatenate(halves, axis=1))
        solved = from_left(right_x_ref, spectrum * jnp.concatenate([weight, weight], axis=0))
        for k in range(2):
            flat_out[pl.ds(y + k, rows, stride=columns), :] = solved[:, k * lanes:(k + 1) * lanes]
    inverse_kernel(
        number, plan, in_ref.at[:, pl.ds(2, 2)], u_ref, v_ref, w_ref, left_ref, right_ref, own_ref, back_ref
    )


def add_kernel(plan, more_ref, sum_ref, total_ref):
    total_ref[...] = sum_ref[...] + more_ref[...]


def in_hbm(value):
    return pltpu.with_memory_space_constraint(value, pltpu.HBM)


def as_it_comes(arrived):
    return arrived if arrived.shape[1] == 2 else in_hbm(arrived)


def params():
    return pltpu.CompilerParams(dimension_semantics=("arbitrary",), vmem_limit_bytes=VMEM_BYTES)


def whole(shape):
    return pl.BlockSpec(shape, lambda *_: (0,) * len(shape))


def part(shape, place):
    return pl.BlockSpec((shape[0], 2) + shape[2:], lambda *_: (0, place, 0, 0, 0))


def orbital_block(shape, number, field):
    return pl.BlockSpec((1,) + shape[1:], lambda i, plan: (plan[number * ENTRY + field], 0, 0, 0))


def forward(number, width, plan, u, orbitals, right, left):
    planes, size, lanes = u.shape
    blocks = lax.axis_size("grid")
    shape = (blocks, 2 * width, planes, size // blocks, lanes)
    return pl.pallas_call(
        lambda *refs: forward_kernel(number, *refs),
        grid_spec=pltpu.PrefetchScalarGridSpec(
            num_scalar_prefetch=1,
            grid=(1,),
            in_specs=[
                whole(u.shape),
                orbital_block(orbitals.shape, number, 0),
                orbital_block(orbitals.shape, number, 1),
                whole(right.shape),
                whole(left.shape),
            ],
            out_specs=part(shape, 0),
        ),
        out_shape=pltpu.HBM(shape, jnp.float32),
        cost_estimate=EARLY if number else None,
        compiler_params=params(),
        name="forward_planes",
    )(plan, u, orbitals, orbitals, right, left)


def solve(arrived, kernel, left, right, ahead=None):
    hbm = pl.BlockSpec(memory_space=pl.ANY)
    operands = [as_it_comes(arrived), kernel, left, right]
    specs = [part(arrived.shape, 0), whole(kernel.shape), whole(left.shape), whole(right.shape)]
    if ahead is None:
        shape, place, aliases = (arrived.shape[0], 2) + arrived.shape[2:], 0, {}
    else:
        shape, place, aliases = ahead.shape, 1, {len(operands): 0}
        operands.append(in_hbm(ahead))
        specs.append(hbm)
    return pl.pallas_call(
        solve_kernel,
        grid=(1,),
        in_specs=specs,
        out_specs=part(shape, place),
        out_shape=pltpu.HBM(shape, jnp.float32),
        input_output_aliases=aliases,
        compiler_params=params(),
        name="solve_columns",
    )(*operands)


def inverse(number, place, plan, arrived, u, orbitals, left, right):
    own = (2,) + u.shape
    return pl.pallas_call(
        lambda *refs: inverse_kernel(number, *refs),
        grid_spec=pltpu.PrefetchScalarGridSpec(
            num_scalar_prefetch=1,
            grid=(1,),
            in_specs=[
                part(arrived.shape, place),
                whole(u.shape),
                orbital_block(orbitals.shape, number, 0),
                orbital_block(orbitals.shape, number, 1),
                whole(left.shape),
                whole(right.shape),
            ],
            out_specs=[whole(own), whole(u.shape)],
        ),
        out_shape=[pltpu.HBM(own, jnp.float32), pltpu.HBM(u.shape, jnp.float32)],
        compiler_params=params(),
        name="inverse_planes",
    )(plan, as_it_comes(arrived), u, orbitals, orbitals, left, right)


def solve_and_inverse(number, plan, arrived, kernel, left_x, right_x, u, orbitals, left, right):
    own = (2,) + u.shape
    field = (arrived.shape[0], 2) + arrived.shape[2:]
    return pl.pallas_call(
        lambda *refs: solve_and_inverse_kernel(number, *refs),
        grid_spec=pltpu.PrefetchScalarGridSpec(
            num_scalar_prefetch=1,
            grid=(1,),
            in_specs=[
                whole(arrived.shape),
                whole(kernel.shape),
                whole(left_x.shape),
                whole(right_x.shape),
                whole(u.shape),
                orbital_block(orbitals.shape, number, 0),
                orbital_block(orbitals.shape, number, 1),
                whole(left.shape),
                whole(right.shape),
            ],
            out_specs=[whole(field), whole(own), whole(u.shape)],
        ),
        out_shape=[
            pltpu.HBM(field, jnp.float32), pltpu.HBM(own, jnp.float32), pltpu.HBM(u.shape, jnp.float32)
        ],
        compiler_params=params(),
        name="solve_and_inverse",
    )(plan, in_hbm(arrived), kernel, left_x, right_x, u, orbitals, orbitals, left, right)


def add_into(number, field, plan, total, more):
    count = more.shape[0]
    one = (1,) + more.shape[1:]
    target = pl.BlockSpec(one, lambda i, plan: (plan[number * ENTRY + field + i], 0, 0, 0))
    return pl.pallas_call(
        add_kernel,
        grid_spec=pltpu.PrefetchScalarGridSpec(
            num_scalar_prefetch=1,
            grid=(count,),
            in_specs=[pl.BlockSpec(one, lambda i, plan: (i, 0, 0, 0)), target],
            out_specs=target,
        ),
        out_shape=jax.ShapeDtypeStruct(total.shape, jnp.float32),
        input_output_aliases={2: 0},
        compiler_params=params(),
        name="add_terms",
    )(plan, more, total)


def signed(number, length):
    return jnp.where(number < length // 2, number, number - length)


def coulomb_block(size, column_count, first_column):
    strength = math.sqrt(size**3) / 4.0
    along_x = signed(jnp.arange(size, dtype=jnp.int32), size)
    along_y = signed(first_column + jnp.arange(column_count, dtype=jnp.int32), size)
    squared = along_y[:, None, None] ** 2 + along_x[None, :, None] ** 2 + along_x[None, None, :] ** 2
    bounded = jnp.maximum(squared, 1).astype(jnp.float32)
    kernel = jnp.where(squared == 0, jnp.float32(0.0), jnp.float32(strength) / bounded)
    return kernel * jnp.float32(1.0 / size**3)


def exchange(field):
    return lax.all_to_all(field, "grid", split_axis=0, concat_axis=0, tiled=True)


def to_partner(value):
    pairs = [(g, g ^ (1 << PARTNER_BIT)) for g in range(lax.axis_size("band"))]
    return lax.ppermute(value, "band", pairs)


def sent_orbital(number, plan, orbitals):
    return lax.dynamic_index_in_dim(orbitals, plan[number * ENTRY + 4], 0, keepdims=False)


def in_rounds(rounds, plan, received, orbitals, kernel, sends, tables):
    plus, plus_x, minus, minus_x = tables
    us = [received]
    for number in range(1, rounds):
        sent, us[-1] = lax.optimization_barrier((sends[number - 1], us[-1]))
        us.append(to_partner(sent))

    def planes_of(number):
        return forward(number, 1 if number == 0 else 2, plan, us[number], orbitals, minus, plus)

    total = jnp.zeros_like(orbitals)
    returned, owns = [], []

    def give(own, back):
        owns.append(own)
        returned.append(to_partner(back))

    arrived = exchange(planes_of(0))
    for number in range(rounds - 1):
        leaving = solve(arrived, kernel, plus_x, minus_x, planes_of(number + 1))
        if number > 1:
            leaving, returned[number - 2] = lax.optimization_barrier((leaving, returned[number - 2]))
        arrived = exchange(leaving)
        if number < rounds - 2:
            give(*inverse(number, 1, plan, arrived, us[number], orbitals, minus, plus))
    leaving, own, back = solve_and_inverse(
        rounds - 2, plan, arrived, kernel, plus_x, minus_x, us[rounds - 2], orbitals, minus, plus
    )
    leaving, returned[rounds - 3] = lax.optimization_barrier((leaving, returned[rounds - 3]))
    arrived = exchange(leaving)
    give(own, back)
    give(*inverse(rounds - 1, 0, plan, arrived, us[rounds - 1], orbitals, minus, plus))
    for number in range(rounds):
        total = add_into(number, 0, plan, total, owns[number])
        if number > 0:
            total = add_into(number - 1, 4, plan, total, returned[number - 1][None])
    place = plan[(rounds - 1) * ENTRY + 4]
    last = lax.dynamic_index_in_dim(total, place, 0, keepdims=False) + returned[-1]
    return lax.dynamic_update_index_in_dim(total, last, place, 0)


def shards(orbitals, spin_channel):
    count, planes, size, lanes = orbitals.shape
    column_count = size // lax.axis_size("grid")
    plan, sent = make_plan(spin_channel, orbitals)
    received = to_partner(sent)
    sends = [sent_orbital(number, plan, orbitals) for number in range(1, ROUNDS + 1)]
    kernel = coulomb_block(size, column_count, lax.axis_index("grid") * column_count)
    tables = tuple(two_parts(t) for t in fourier_tables(size, planes))
    more, kernel, sends = lax.optimization_barrier((needs_more(spin_channel), kernel, sends))
    return lax.cond(
        more,
        lambda *args: in_rounds(ROUNDS + 1, *args, tables),
        lambda *args: in_rounds(ROUNDS, *args, tables),
        plan, received, orbitals, kernel, sends,
    )


def solution(mesh):
    return jax.shard_map(
        shards,
        mesh=mesh,
        in_specs=(P("band", "grid", None, None), P()),
        out_specs=P("band", "grid", None, None),
        check_vma=False,
    )
```
